1024 devices in a mesh: expert: 32 (over z_hi, x, core), dp: 32 (over z_lo, y).
Axes of the slice: x: 4, y: 8, z: 16 (z_hi: 4, z_lo: 4; z = z_hi * 4 + z_lo), core: 2. Of those that a mesh axis runs over, the one named last changes fastest.
Arguments:
- tokens: bfloat16 [256, 256, 640], P('dp', None, 'expert'), may hold values from -40 to 40
- slot_params: bfloat16 [640, 128], P('expert'), may hold values from -40 to 40
- w_in: bfloat16 [128, 640, 5120], P('expert', None, 'dp'), may hold values from -0.25 to 0.25
- w_out: bfloat16 [128, 5120, 640], P('expert', 'dp'), may hold values from -0.078125 to 0.078125
- out_grad: bfloat16 [256, 256, 640], P('dp', None, 'expert'), may hold values from -6 to 6
Outputs:
- grad_tokens: bfloat16 [256, 256, 640], P('dp', None, 'expert')
- grad_w_in: bfloat16 [128, 640, 5120], P('expert', None, 'dp')
- grad_w_out: bfloat16 [128, 5120, 640], P('expert', 'dp')
The draws below stay inside these ranges and needn't reach their ends.
All inputs are finite; a program needn't handle non-finite values.
Results may differ from the reference program's by a relative error of at most 0.034.
Values may be sent and summed in bfloat16 or wider, within the bound.
A program may use at most 32 MiB of HBM per device.

```python
import math
import jax
import jax.numpy as jnp
from jax import lax

D = 640
F = 5120
PATCHES = 256
EXPERTS = 128
SLOTS = 128
IMAGES = 256
N_DP = 32


def scaled_field(key, shape, scale_shape):
    k_base, k_scale = jax.random.split(key, 2)
    base = jnp.clip(jax.random.normal(k_base, shape, jnp.float32), -4.0, 4.0)
    spread = math.log(10.0)
    factor = jnp.exp(jax.random.uniform(k_scale, scale_shape, jnp.float32, 0.0, spread))
    return (base * factor).astype(jnp.bfloat16)


def draw_tokens(key, part):
    key = jax.random.fold_in(key, 11)
    return scaled_field(key, (IMAGES, PATCHES, D), (IMAGES, PATCHES, 1))


def draw_slot_params(key, part):
    key = jax.random.fold_in(key, 23)
    return scaled_field(key, (D, SLOTS), (1, SLOTS))


def block_scale(rng, dims, cuts, smallest, top_value):
    factor_of = 1.0
    for position, parts in cuts:
        draws = jax.random.uniform(jax.random.fold_in(jax.random.fold_in(rng, 6), position), (parts,), jnp.float32, smallest / len(cuts), top_value / len(cuts))
        factor_of = factor_of * jnp.repeat(jnp.exp(draws), dims[position] // parts).reshape((-1,) + (1,) * (len(dims) - 1 - position))
    return factor_of


def gaussian(key, extent, scale, most, shards=(), kind=jnp.bfloat16):
    factor_of = block_scale(key, extent, shards, -0.22, 0.18) if shards else 1.0
    entries = jax.random.normal(key, extent, jnp.float32) * scale * factor_of
    return jnp.minimum(jnp.maximum(entries, -most), most).astype(kind)


def setup_inputs(seed: int = 0) -> dict:
    key_list = jax.random.split(jax.random.key(seed), 6)
    tokens = draw_tokens(jax.random.fold_in(key_list[5], 71), 0)
    slot_params = draw_slot_params(jax.random.fold_in(key_list[5], 71), 0)
    w_in = gaussian(key_list[2], (EXPERTS, D, F), D ** -0.5, 0.25, ((0, 32), (2, 32)))
    w_out = gaussian(key_list[3], (EXPERTS, F, D), F ** -0.5, 0.078125, ((0, 32), (1, 32)))
    out_grad = gaussian(key_list[4], (IMAGES, PATCHES, D), 1.0, 6.0, ((0, 32), (2, 32)))
    return dict(tokens=tokens, slot_params=slot_params, w_in=w_in, w_out=w_out, out_grad=out_grad)


SCALE = 32.0
EPS = 1e-06

def block_sum(left, right):
    count = left.shape[0]
    width = right.shape[1]
    left_blocks = left.reshape(count, N_DP, -1).astype(jnp.float32)
    right_blocks = right.reshape(N_DP, -1, width).astype(jnp.float32)
    partial_sums = jnp.einsum('inf,nfd->nid', left_blocks, right_blocks).astype(jnp.bfloat16)
    partial_sums = lax.optimization_barrier(partial_sums)
    return lax.optimization_barrier(jnp.sum(partial_sums.astype(jnp.float32), 0)).astype(jnp.bfloat16)

def expert_step(packed):
    rows, grads, first, second = packed
    hidden = jnp.dot(rows, first, preferred_element_type=jnp.float32)
    act_b = jax.nn.gelu(hidden).astype(jnp.bfloat16)
    slot_out = block_sum(act_b, second)
    dact = jnp.dot(grads, second.T, preferred_element_type=jnp.float32)
    _, pull = jax.vjp(jax.nn.gelu, hidden)
    dhid = pull(dact)[0].astype(jnp.bfloat16)
    grad_second = jnp.dot(act_b.T, grads, preferred_element_type=jnp.float32).astype(jnp.bfloat16)
    grad_first = jnp.dot(rows.T, dhid, preferred_element_type=jnp.float32).astype(jnp.bfloat16)
    slot_back = block_sum(dhid, first.T)
    return (slot_out, slot_back, grad_first, grad_second)

def reference(tokens, slot_params, w_in, w_out, out_grad):
    xfull = tokens.astype(jnp.float32)
    pfull = slot_params.astype(jnp.float32)
    gfull = out_grad.astype(jnp.float32)
    prod = jnp.einsum('imd,ds->ims', xfull, pfull)
    row_inv = lax.rsqrt(lax.optimization_barrier(jnp.sum(xfull * xfull, -1)) + EPS)
    col_inv = lax.rsqrt(lax.optimization_barrier(jnp.sum(pfull * pfull, 0)) + EPS)
    logits = SCALE * prod * row_inv[:, :, None] * col_inv[None, None, :]
    expo = jnp.exp(logits)
    dispatch = expo / lax.optimization_barrier(jnp.sum(expo, 1, keepdims=True))
    combine = expo / lax.optimization_barrier(jnp.sum(expo, 2, keepdims=True))
    dispatch_b = dispatch.astype(jnp.bfloat16)
    combine_b = combine.astype(jnp.bfloat16)
    slot_in = jnp.einsum('ims,imd->isd', dispatch_b.astype(jnp.float32), xfull).astype(jnp.bfloat16)
    slot_grad = jnp.einsum('ims,imd->isd', combine_b.astype(jnp.float32), gfull).astype(jnp.bfloat16)
    slot_out, slot_back, grad_w_in, grad_w_out = lax.map(expert_step, (jnp.transpose(slot_in, (1, 0, 2)), jnp.transpose(slot_grad, (1, 0, 2)), w_in, w_out))
    slot_out = jnp.transpose(slot_out, (1, 0, 2)).astype(jnp.float32)
    slot_back = jnp.transpose(slot_back, (1, 0, 2)).astype(jnp.float32)
    dcomb = jnp.einsum('imd,isd->ims', gfull, slot_out)
    ddisp = jnp.einsum('imd,isd->ims', xfull, slot_back)
    dlog = combine * (dcomb - lax.optimization_barrier(jnp.sum(combine * dcomb, 2, keepdims=True)))
    dlog = dlog + dispatch * (ddisp - lax.optimization_barrier(jnp.sum(dispatch * ddisp, 1, keepdims=True)))
    centre = lax.optimization_barrier(jnp.sum(dlog * logits, 2))
    pulled = (SCALE * dlog * col_inv[None, None, :]).astype(jnp.bfloat16)
    backward = jnp.einsum('ims,ds->imd', pulled.astype(jnp.float32), pfull)
    direct = jnp.einsum('ims,isd->imd', dispatch_b.astype(jnp.float32), slot_back)
    grad_tokens = direct + row_inv[:, :, None] * (backward - xfull * (row_inv * centre)[:, :, None])
    return (grad_tokens.astype(jnp.bfloat16), grad_w_in, grad_w_out)
```

```python
import functools

import jax
import jax.numpy as jnp
from jax import lax
from jax.experimental import pallas as pl
from jax.experimental.pallas import tpu as pltpu
from jax.sharding import PartitionSpec as P

SCALE = 32.0
EPS = 1e-06
MESH = pl.DeviceIdType.MESH
BF = jnp.bfloat16
F32 = jnp.float32
NZ, NY = 4, 8


def spread_kernel(n, per, x_ref, y_ref, local_sem, send_sem, recv_sem):
    me = lax.axis_index("expert")
    barrier = pltpu.get_barrier_semaphore()

    def greet(k, carry):
        pl.semaphore_signal(
            barrier, inc=1, device_id={"expert": lax.rem(me + k, n)}, device_id_type=MESH
        )
        return carry

    def copy(k):
        to = lax.rem(me + k, n)
        return pltpu.make_async_remote_copy(
            src_ref=x_ref.at[lax.div(to, per)],
            dst_ref=y_ref.at[me],
            send_sem=send_sem.at[k],
            recv_sem=recv_sem.at[k],
            device_id={"expert": to},
            device_id_type=MESH,
        )

    def start(k, carry):
        copy(k).start()
        return carry

    def finish(k, carry):
        copy(k).wait()
        return carry

    lax.fori_loop(1, n, greet, 0)
    own = pltpu.make_async_copy(x_ref.at[lax.div(me, per)], y_ref.at[me], local_sem)
    own.start()
    pl.semaphore_wait(barrier, n - 1)
    lax.fori_loop(1, n, start, 0)
    own.wait()
    lax.fori_loop(1, n, finish, 0)


def spread(x, n, per, collective_id):
    return pl.pallas_call(
        functools.partial(spread_kernel, n, per),
        out_shape=jax.ShapeDtypeStruct((n,) + x.shape[1:], x.dtype),
        in_specs=[pl.BlockSpec(memory_space=pltpu.VMEM)],
        out_specs=pl.BlockSpec(memory_space=pltpu.VMEM),
        scratch_shapes=[
            pltpu.SemaphoreType.DMA,
            pltpu.SemaphoreType.DMA((n,)),
            pltpu.SemaphoreType.DMA((n,)),
        ],
        compiler_params=pltpu.CompilerParams(
            collective_id=collective_id, has_side_effects=True, vmem_limit_bytes=24 * 2**20
        ),
    )(x)


def place():
    p = lax.axis_index("dp")
    return lax.div(p, NY), lax.rem(p, NY)


def at(z, y):
    return lax.rem(z, NZ) * NY + lax.rem(y, NY)


def greet_grid(z, y):
    barrier = pltpu.get_barrier_semaphore()
    others = [at(z, y + 1), at(z, y + NY - 1)] + [at(z + k, y) for k in range(1, NZ)]
    for other in others:
        pl.semaphore_signal(barrier, inc=1, device_id={"dp": other}, device_id_type=MESH)
    pl.semaphore_wait(barrier, len(others))


def gather_kernel(b_ref, y_ref, local_sem, z_send, z_recv, y_send, y_recv):
    z, y = place()
    p = at(z, y)
    greet_grid(z, y)
    own = pltpu.make_async_copy(b_ref, y_ref.at[:, p], local_sem)
    own.start()

    def z_copy(k):
        return pltpu.make_async_remote_copy(
            src_ref=b_ref,
            dst_ref=y_ref.at[:, p],
            send_sem=z_send.at[k],
            recv_sem=z_recv.at[k],
            device_id={"dp": at(z + k, y)},
            device_id_type=MESH,
        )

    def y_copy(chain, step, way):
        back = NY - (step - 1) if way == 0 else step - 1
        slot = at(z + chain, y + back)
        rows = pl.ds(0, 8) if step < NY // 2 else pl.ds(4 * way, 4)
        src = b_ref if chain == 0 and step == 1 else y_ref.at[:, slot]
        return pltpu.make_async_remote_copy(
            src_ref=src.at[rows],
            dst_ref=y_ref.at[rows, slot],
            send_sem=y_send.at[chain, step, way],
            recv_sem=y_recv.at[chain, step, way],
            device_id={"dp": at(z, y + (1 if way == 0 else NY - 1))},
            device_id_type=MESH,
        )

    z_copies = {k: z_copy(k) for k in (3, 1, 2)}
    y_copies = {}
    for way in (0, 1):
        y_copies[0, 1, way] = y_copy(0, 1, way)
        y_copies[0, 1, way].start()
    for k in (3, 1, 2):
        z_copies[k].start()
    for chain in (1, 3, 2):
        z_copies[NZ - chain].wait_recv()
        for way in (0, 1):
            y_copies[chain, 1, way] = y_copy(chain, 1, way)
            y_copies[chain, 1, way].start()
    for step in range(2, NY // 2 + 1):
        for chain in (0, 1, 3, 2):
            for way in (0, 1):
                y_copies[chain, step - 1, way].wait_recv()
                y_copies[chain, step, way] = y_copy(chain, step, way)
                y_copies[chain, step, way].start()
    for chain in (0, 1, 3, 2):
        for way in (0, 1):
            y_copies[chain, NY // 2, way].wait_recv()
    own.wait()
    for copy in z_copies.values():
        copy.wait_send()
    for copy in y_copies.values():
        copy.wait_send()


def gather(block, collective_id):
    a, j, d = block.shape
    return pl.pallas_call(
        gather_kernel,
        out_shape=jax.ShapeDtypeStruct((a, NZ * NY, j, d), block.dtype),
        in_specs=[pl.BlockSpec(memory_space=pltpu.VMEM)],
        out_specs=pl.BlockSpec(memory_space=pltpu.VMEM),
        scratch_shapes=[
            pltpu.SemaphoreType.DMA,
            pltpu.SemaphoreType.DMA((NZ,)),
            pltpu.SemaphoreType.DMA((NZ,)),
            pltpu.SemaphoreType.DMA((NZ, NY // 2 + 1, 2)),
            pltpu.SemaphoreType.DMA((NZ, NY // 2 + 1, 2)),
        ],
        compiler_params=pltpu.CompilerParams(
            collective_id=collective_id, has_side_effects=True, vmem_limit_bytes=32 * 2**20
        ),
    )(block)


def scatter_kernel(p_ref, o_ref, ring, total, z_out, z_in, z_send, z_recv, y_send, y_recv):
    z, y = place()
    greet_grid(z, y)
    half = NY // 2

    def y_copy(chain, step, way):
        slot = at(z + chain, y + (step if way == 0 else NY - step))
        rows = pl.ds(4 * way, 4) if step == half else pl.ds(0, 8)
        src = p_ref.at[:, slot] if step == half else ring.at[chain, step, way]
        return pltpu.make_async_remote_copy(
            src_ref=src.at[rows],
            dst_ref=ring.at[chain, step - 1, way, rows],
            send_sem=y_send.at[chain, step, way],
            recv_sem=y_recv.at[chain, step, way],
            device_id={"dp": at(z, y + (1 if way == 0 else NY - 1))},
            device_id_type=MESH,
        )

    def z_copy(chain):
        return pltpu.make_async_remote_copy(
            src_ref=z_out.at[chain],
            dst_ref=z_in.at[chain],
            send_sem=z_send.at[chain],
            recv_sem=z_recv.at[chain],
            device_id={"dp": at(z + chain, y)},
            device_id_type=MESH,
        )

    order = (1, 3, 2, 0)
    y_copies, z_copies = {}, {}
    for chain in order:
        for way in (0, 1):
            y_copies[chain, half, way] = y_copy(chain, half, way)
            y_copies[chain, half, way].start()
    for step in range(half - 1, 0, -1):
        for chain in order:
            for way in (0, 1):
                y_copies[chain, step + 1, way].wait_recv()
                slot = at(z + chain, y + (step if way == 0 else NY - step))
                for a in range(8):
                    mine = p_ref[a, slot]
                    if step < half - 1 or a // 4 == way:
                        mine = (mine.astype(F32) + ring[chain, step, way, a].astype(F32)).astype(BF)
                    ring[chain, step, way, a] = mine
                y_copies[chain, step, way] = y_copy(chain, step, way)
                y_copies[chain, step, way].start()
    here = [at(z + chain, y) for chain in range(NZ)]
    for chain in order:
        for way in (0, 1):
            y_copies[chain, 1, way].wait_recv()
        for a in range(8):
            summed = (
                p_ref[a, here[chain]].astype(F32)
                + ring[chain, 0, 0, a].astype(F32)
                + ring[chain, 0, 1, a].astype(F32)
            )
            if chain == 0:
                total[a] = summed
            else:
                z_out[chain, a] = summed.astype(BF)
        if chain != 0:
            z_copies[chain] = z_copy(chain)
            z_copies[chain].start()
    for chain in (1, 3, 2):
        z_copies[chain].wait_recv()
    for a in range(8):
        o_ref[a] = (
            total[a]
            + z_in[1, a].astype(F32)
            + z_in[2, a].astype(F32)
            + z_in[3, a].astype(F32)
        )
    for copy in z_copies.values():
        copy.wait_send()
    for copy in y_copies.values():
        copy.wait_send()


def scatter(parts, collective_id):
    a, _, j, d = parts.shape
    return pl.pallas_call(
        scatter_kernel,
        out_shape=jax.ShapeDtypeStruct((a, j, d), F32),
        in_specs=[pl.BlockSpec(memory_space=pltpu.VMEM)],
        out_specs=pl.BlockSpec(memory_space=pltpu.VMEM),
        scratch_shapes=[
            pltpu.VMEM((NZ, NY // 2, 2, a, j, d), BF),
            pltpu.VMEM((a, j, d), F32),
            pltpu.VMEM((NZ, a, j, d), BF),
            pltpu.VMEM((NZ, a, j, d), BF),
            pltpu.SemaphoreType.DMA((NZ,)),
            pltpu.SemaphoreType.DMA((NZ,)),
            pltpu.SemaphoreType.DMA((NZ, NY // 2 + 1, 2)),
            pltpu.SemaphoreType.DMA((NZ, NY // 2 + 1, 2)),
        ],
        compiler_params=pltpu.CompilerParams(
            collective_id=collective_id, has_side_effects=True, vmem_limit_bytes=40 * 2**20
        ),
    )(parts)


def three(x):
    hi = lax.reduce_precision(x, 8, 7)
    mid = lax.reduce_precision(x - hi, 8, 7)
    low = x - hi - mid
    packed = jnp.stack([hi, mid, low], -1).astype(BF)
    return jnp.pad(packed, [(0, 0)] * x.ndim + [(0, 125)])


def joined(packed):
    return packed[..., 0].astype(F32) + packed[..., 1].astype(F32) + packed[..., 2].astype(F32)


def local(n, tokens, slot_params, w_in, w_out, out_grad):
    images, patches, feats = tokens.shape
    per = n // images
    m = patches // per
    slots = slot_params.shape[1]
    d = n * feats
    own = slots // n

    def cut(x):
        return jnp.transpose(x.reshape(images, per, m, feats), (0, 1, 3, 2)).reshape(n, feats, m)

    packed = jnp.concatenate(
        [cut(tokens), cut(out_grad), jnp.broadcast_to(slot_params, (n, feats, slots))], 2
    )
    packed = spread(packed, n, 1, 0).reshape(d, 2 * m + slots)
    x, g, params = packed[:, :m], packed[:, m : 2 * m], packed[:, 2 * m :]

    xf = x.astype(F32)
    pf = params.astype(F32)
    prod = jnp.einsum("dm,ds->ms", x, params, preferred_element_type=F32)
    row_inv = lax.rsqrt(jnp.sum(xf * xf, 0) + EPS)
    col_inv = lax.rsqrt(jnp.sum(pf * pf, 0) + EPS)
    logits = SCALE * prod * row_inv[:, None] * col_inv[None, :]
    expo = jnp.exp(logits)
    combine = expo / jnp.sum(expo, 1, keepdims=True)
    part_in = jnp.einsum("ms,dm->sd", expo.astype(BF), x, preferred_element_type=F32)
    part_grad = jnp.einsum("ms,dm->sd", combine.astype(BF), g, preferred_element_type=F32)
    part_den = jnp.sum(expo, 0)

    rows = jnp.concatenate([part_in.astype(BF), three(part_den)], 1).reshape(n, own, d + 128)
    grads = jnp.pad(part_grad.astype(BF), [(0, 0), (0, 128)]).reshape(n, own, d + 128)
    parts = spread(jnp.concatenate([rows, grads], 1), n, 1, 1)
    parts = parts.reshape(images, per, 2 * own, d + 128)
    den = jnp.sum(joined(parts[:, :, :own, d:]), 1)
    sums = jnp.sum(parts[..., :d].astype(F32), 1)
    slot_in = jnp.transpose(sums[:, :own] / den[:, :, None], (1, 0, 2))
    slot_grad = jnp.transpose(sums[:, own:], (1, 0, 2))
    block = jnp.concatenate([slot_in, slot_grad], 0).astype(BF)

    every = gather(block, 2).reshape(2 * own, -1, d)
    xs, gs = every[:own], every[own:]
    hidden = jnp.einsum("end,edf->enf", xs, w_in, preferred_element_type=F32)
    act_b = jax.nn.gelu(hidden).astype(BF)
    out_part = jnp.einsum("enf,efd->end", act_b, w_out, preferred_element_type=F32)
    dact = jnp.einsum("end,efd->enf", gs, w_out, preferred_element_type=F32)
    _, pull = jax.vjp(jax.nn.gelu, hidden)
    dhid = pull(dact)[0].astype(BF)
    back_part = jnp.einsum("enf,edf->end", dhid, w_in, preferred_element_type=F32)
    summed = jnp.concatenate([out_part.astype(BF), back_part.astype(BF)], 0)
    summed = scatter(summed.reshape(2 * own, -1, images, d), 3)
    grad_w_out = jnp.einsum("enf,end->efd", act_b, gs, preferred_element_type=F32).astype(BF)
    grad_w_in = jnp.einsum("end,enf->edf", xs, dhid, preferred_element_type=F32).astype(BF)

    summed = jnp.transpose(summed, (1, 0, 2))
    slot_back = summed[:, own:].astype(BF)
    mean = jnp.sum(jnp.transpose(slot_in, (1, 0, 2)) * slot_back.astype(F32), 2)
    extra = three(jnp.concatenate([1.0 / den, mean], 1))
    results = jnp.concatenate([summed.astype(BF), extra], 2)
    results = spread(results, n, per, 4)
    slot_out = results[:, :own, :d].reshape(slots, d)
    slot_back = results[:, own:, :d].reshape(slots, d)
    den_inv = joined(results[:, :own, d:]).reshape(slots)
    mean = joined(results[:, own:, d:]).reshape(slots)

    dispatch = expo * den_inv[None, :]
    dcomb = jnp.einsum("dm,sd->ms", g, slot_out, preferred_element_type=F32)
    ddisp = jnp.einsum("dm,sd->ms", x, slot_back, preferred_element_type=F32)
    dlog = combine * (dcomb - jnp.sum(combine * dcomb, 1, keepdims=True))
    dlog = dlog + dispatch * (ddisp - mean[None, :])
    centre = jnp.sum(dlog * logits, 1)
    pulled = (SCALE * dlog * col_inv[None, :]).astype(BF)
    backward = jnp.einsum("ms,ds->dm", pulled, params, preferred_element_type=F32)
    direct = jnp.einsum("ms,sd->dm", dispatch.astype(BF), slot_back, preferred_element_type=F32)
    grad = direct + row_inv[None, :] * (backward - xf * (row_inv * centre)[None, :])
    grad = spread(grad.astype(BF).reshape(n, feats, m), n, 1, 5)
    grad = jnp.transpose(grad.reshape(images, per, feats, m), (0, 1, 3, 2))
    return (grad.reshape(images, patches, feats), grad_w_in, grad_w_out)


def solution(mesh):
    return jax.shard_map(
        functools.partial(local, mesh.shape["expert"]),
        mesh=mesh,
        in_specs=(
            P("dp", None, "expert"),
            P("expert", None),
            P("expert", None, "dp"),
            P("expert", "dp", None),
            P("dp", None, "expert"),
        ),
        out_specs=(P("dp", None, "expert"), P("expert", None, "dp"), P("expert", "dp", None)),
        check_vma=False,
    )
```

```python
import functools

import jax
import jax.numpy as jnp
from jax import lax
from jax.experimental import pallas as pl
from jax.experimental.pallas import tpu as pltpu
from jax.sharding import PartitionSpec as P

SCALE = 32.0
EPS = 1e-06
MESH = pl.DeviceIdType.MESH
BF = jnp.bfloat16
F32 = jnp.float32
NZ, NY = 4, 8
NE = 32
IM = NE // 4
D = 640
EXTRA = 128
NT = (((1,), (1,)), ((), ()))
TN = (((0,), (0,)), ((), ()))


def mm(a, b, dims=(((1,), (0,)), ((), ()))):
    return lax.dot_general(a, b, dims, preferred_element_type=F32)


def at(z, y):
    return lax.rem(z, NZ) * NY + lax.rem(y, NY)


def team(j, q):
    return lax.rem(j, IM) * 4 + lax.rem(q, 4)


def send(src, dst, send_sem, recv_sem, **to):
    copy = pltpu.make_async_remote_copy(
        src_ref=src,
        dst_ref=dst,
        send_sem=send_sem,
        recv_sem=recv_sem,
        device_id=to,
        device_id_type=MESH,
    )
    return copy


def three(x, lane, first):
    hi = x.astype(BF).astype(F32)
    mid = (x - hi).astype(BF).astype(F32)
    low = x - hi - mid
    zero = jnp.zeros_like(x)
    return jnp.where(
        lane == first,
        hi,
        jnp.where(lane == first + 1, mid, jnp.where(lane == first + 2, low, zero)),
    )


def greet(me, z, y):
    barrier = pltpu.get_barrier_semaphore()

    def one(k, carry):
        pl.semaphore_signal(
            barrier, inc=1, device_id={"expert": lax.rem(me + k, NE)}, device_id_type=MESH
        )
        return carry

    lax.fori_loop(1, NE, one, 0)
    others = [at(z, y + 1), at(z, y + NY - 1)] + [at(z + k, y) for k in range(1, NZ)]
    for other in others:
        pl.semaphore_signal(barrier, inc=1, device_id={"dp": other}, device_id_type=MESH)
    pl.semaphore_wait(barrier, NE - 1 + len(others))


def spread(x_ref, y_ref, sems):
    me = lax.axis_index("expert")
    send_sem, recv_sem = sems

    def copy(k):
        to = lax.rem(me + k, NE)
        return send(x_ref.at[to], y_ref.at[me], send_sem.at[k], recv_sem.at[k], expert=to)

    def start(k, carry):
        copy(k).start()
        return carry

    def finish(k, carry):
        copy(k).wait()
        return carry

    lax.fori_loop(1, NE, start, 0)
    y_ref[me] = x_ref[me]
    return lambda: lax.fori_loop(1, NE, finish, 0)


def share_along(w_ref, v_ref, sems):
    me = lax.axis_index("expert")
    hi, lo = lax.div(me, 8), lax.rem(me, 8)
    copies = []
    for k in range(1, 4):
        to = lax.rem(hi + k, 4) * 8 + lo
        copies.append(
            send(w_ref, v_ref.at[hi, lo], sems[0].at[k], sems[1].at[k], expert=to)
        )
        copies[-1].start()
    v_ref[hi, lo] = w_ref[...]
    return copies


def share_across(v_ref, sems):
    me = lax.axis_index("expert")
    hi, lo = lax.div(me, 8), lax.rem(me, 8)
    copies = []
    for k in range(1, 8):
        to = hi * 8 + lax.rem(lo + k, 8)
        copies.append(
            send(v_ref.at[:, lo], v_ref.at[:, lo], sems[0].at[k], sems[1].at[k], expert=to)
        )
        copies[-1].start()
    return copies


def collect(x_ref, o_ref, part, total, q_sems, j_sems):
    me = lax.axis_index("expert")
    j, q = lax.div(me, 4), lax.rem(me, 4)
    q_copies, j_copies = {}, {}
    steps = list(range(1, IM)) + [0]
    for step in steps:
        to = lax.rem(j + step, IM)
        for k in range(1, 4):
            q_copies[step, k] = send(
                x_ref.at[lax.rem(q + k, 4), to],
                part.at[k, step],
                q_sems[0].at[step, k],
                q_sems[1].at[step, k],
                expert=team(j, q + k),
            )
            q_copies[step, k].start()
    for step in steps:
        to = lax.rem(j + step, IM)
        for k in range(1, 4):
            q_copies[step, k].wait_recv()
        summed = x_ref[q, to].astype(F32)
        for k in range(1, 4):
            summed = summed + part[k, step].astype(F32)
        if step == 0:
            o_ref[j] = summed.astype(BF)
            continue
        total[step] = summed.astype(BF)
        j_copies[step] = send(
            total.at[step],
            o_ref.at[j],
            j_sems[0].at[step],
            j_sems[1].at[step],
            expert=team(to, q),
        )
        j_copies[step].start()
    for copy in j_copies.values():
        copy.wait()
    for copy in q_copies.values():
        copy.wait_send()


def give_back(x_ref, o_ref, q_sems, j_sems):
    me = lax.axis_index("expert")
    j, q = lax.div(me, 4), lax.rem(me, 4)
    q_copies, j_copies = {}, {}
    for step in range(1, IM):
        to = lax.rem(j + step, IM)
        j_copies[step] = send(
            x_ref.at[to],
            o_ref.at[q, j],
            j_sems[0].at[step],
            j_sems[1].at[step],
            expert=team(to, q),
        )
        j_copies[step].start()
    o_ref[q, j] = x_ref[j]
    for step in range(IM):
        here = lax.rem(j + IM - step, IM)
        if step:
            j_copies[step].wait_recv()
        for k in range(1, 4):
            q_copies[step, k] = send(
                o_ref.at[q, here],
                o_ref.at[q, here],
                q_sems[0].at[step, k],
                q_sems[1].at[step, k],
                expert=team(j, q + k),
            )
            q_copies[step, k].start()
    for copy in q_copies.values():
        copy.wait()
    for copy in j_copies.values():
        copy.wait_send()


def gather(b_ref, y_ref, z, y, z_sems, y_sems):
    p = at(z, y)

    def y_copy(chain, step, way):
        back = NY - (step - 1) if way == 0 else step - 1
        slot = at(z + chain, y + back)
        rows = pl.ds(0, 8) if step < NY // 2 else pl.ds(4 * way, 4)
        src = b_ref if chain == 0 and step == 1 else y_ref.at[:, slot]
        return send(
            src.at[rows],
            y_ref.at[rows, slot],
            y_sems[0].at[chain, step, way],
            y_sems[1].at[chain, step, way],
            dp=at(z, y + (1 if way == 0 else NY - 1)),
        )

    y_copies, z_copies = {}, {}
    for way in (0, 1):
        y_copies[0, 1, way] = y_copy(0, 1, way)
        y_copies[0, 1, way].start()
    for k in (3, 1, 2):
        z_copies[k] = send(
            b_ref, y_ref.at[:, p], z_sems[0].at[k], z_sems[1].at[k], dp=at(z + k, y)
        )
        z_copies[k].start()
    y_ref[:, p] = b_ref[...]
    for chain in (1, 3, 2):
        z_copies[NZ - chain].wait_recv()
        for way in (0, 1):
            y_copies[chain, 1, way] = y_copy(chain, 1, way)
            y_copies[chain, 1, way].start()
    for step in range(2, NY // 2 + 1):
        for chain in (0, 1, 3, 2):
            for way in (0, 1):
                y_copies[chain, step - 1, way].wait_recv()
                y_copies[chain, step, way] = y_copy(chain, step, way)
                y_copies[chain, step, way].start()
    for chain in (0, 1, 3, 2):
        for way in (0, 1):
            y_copies[chain, NY // 2, way].wait_recv()
    for copy in z_copies.values():
        copy.wait_send()
    for copy in y_copies.values():
        copy.wait_send()


def scatter(p_ref, total, ring, z_out, z_in, z, y, z_sems, y_sems, meanwhile):
    half = NY // 2

    def y_copy(chain, step, way):
        slot = at(z + chain, y + (step if way == 0 else NY - step))
        rows = pl.ds(4 * way, 4) if step == half else pl.ds(0, 8)
        src = p_ref.at[:, slot] if step == half else ring.at[chain, step, way]
        return send(
            src.at[rows],
            ring.at[chain, step - 1, way, rows],
            y_sems[0].at[chain, step, way],
            y_sems[1].at[chain, step, way],
            dp=at(z, y + (1 if way == 0 else NY - 1)),
        )

    order = (1, 3, 2, 0)
    y_copies, z_copies = {}, {}
    for chain in order:
        for way in (0, 1):
            y_copies[chain, half, way] = y_copy(chain, half, way)
            y_copies[chain, half, way].start()
    meanwhile()
    for step in range(half - 1, 0, -1):
        for chain in order:
            for way in (0, 1):
                y_copies[chain, step + 1, way].wait_recv()
                slot = at(z + chain, y + (step if way == 0 else NY - step))
                for a in range(8):
                    mine = p_ref[a, slot]
                    if step < half - 1 or a // 4 == way:
                        mine = (mine.astype(F32) + ring[chain, step, way, a].astype(F32)).astype(BF)
                    ring[chain, step, way, a] = mine
                y_copies[chain, step, way] = y_copy(chain, step, way)
                y_copies[chain, step, way].start()
    for chain in order:
        for way in (0, 1):
            y_copies[chain, 1, way].wait_recv()
        here = at(z + chain, y)
        for a in range(8):
            summed = (
                p_ref[a, here].astype(F32)
                + ring[chain, 0, 0, a].astype(F32)
                + ring[chain, 0, 1, a].astype(F32)
            )
            if chain == 0:
                total[a] = summed
            else:
                z_out[chain, a] = summed.astype(BF)
        if chain != 0:
            z_copies[chain] = send(
                z_out.at[chain],
                z_in.at[chain],
                z_sems[0].at[chain],
                z_sems[1].at[chain],
                dp=at(z + chain, y),
            )
            z_copies[chain].start()
    for chain in (1, 3, 2):
        z_copies[chain].wait_recv()
    for a in range(8):
        total[a] = (
            total[a]
            + z_in[1, a].astype(F32)
            + z_in[2, a].astype(F32)
            + z_in[3, a].astype(F32)
        )
    for copy in z_copies.values():
        copy.wait_send()
    for copy in y_copies.values():
        copy.wait_send()


def whole_kernel(
    x_ref, w_ref, win_ref, wout_ref,
    y_ref, gin_ref, gout_ref,
    xin, vin, xs, ps, parts, part, part_sum, sums, blk, blkb, every, outs, act_s, dhid_s,
    ring, z_out, z_in, total, res, resb, back, chunk,
    s1a, s1b, sa1, sa2, sb1, sb2, cq1, cq2, cj1, cj2, gz1, gz2, gy1, gy2,
    sz1, sz2, sy1, sy2, bq1, bq2, bj1, bj2, s2a, s2b,
):
    me = lax.axis_index("expert")
    quarter = lax.rem(me, 4)
    p = lax.axis_index("dp")
    z, y = lax.div(p, NY), lax.rem(p, NY)
    greet(me, z, y)

    along = share_along(w_ref, vin, (sa1, sa2))
    finish = spread(x_ref, xin, (s1a, s1b))
    for copy in along:
        copy.wait()
    across = share_across(vin, (sb1, sb2))
    finish()
    feats = xin.shape[1]
    for e in range(NE):
        xs[e * feats : (e + 1) * feats, :] = xin[e].astype(F32)
    both = xs[...].T
    both_b = both.astype(BF)
    m = both.shape[0] // 2
    for copy in across:
        copy.wait()
    for e in range(NE):
        ps[e * feats : (e + 1) * feats, :] = vin[e // 8, e % 8].astype(F32)
    params = ps[...]
    params_b = params.astype(BF)

    cols = 2 * NE * 4
    first = (lax.broadcasted_iota(jnp.int32, (1, cols), 1) & 4) == 0
    x = both[:m]
    row_inv = lax.rsqrt(jnp.sum(x * x, 1, keepdims=True) + EPS)
    col_inv = lax.rsqrt(jnp.sum(params * params, 0, keepdims=True) + EPS)
    logits = SCALE * mm(both_b[:m], params_b) * row_inv * col_inv
    expo = jnp.exp(logits)
    combine = expo / (0.5 * jnp.sum(expo, 1, keepdims=True))
    weights = jnp.concatenate([jnp.where(first, expo, 0.0), jnp.where(first, 0.0, combine)], 0).T
    slot_part = mm(weights.astype(BF), both_b)
    lane = lax.broadcasted_iota(jnp.int32, (cols, EXTRA), 1)
    upper = (lax.broadcasted_iota(jnp.int32, (cols, 1), 0) & 4) == 0
    den = jnp.where(upper, jnp.sum(weights, 1, keepdims=True), 0.0)
    den = three(den, lane, 32 * quarter)
    for e in range(NE):
        rows = slice(8 * e, 8 * e + 8)
        parts[e // IM, e % IM, :, :D] = slot_part[rows].astype(BF)
        parts[e // IM, e % IM, :, D:] = den[rows].astype(BF)
    collect(parts, sums, part, part_sum, (cq1, cq2), (cj1, cj2))

    top = lax.broadcasted_iota(jnp.int32, (8, 1), 0) < 4
    for j in range(IM):
        val = sums[j, :, :D].astype(F32)
        den = jnp.sum(sums[j, :, D:].astype(F32), 1, keepdims=True)
        val = val * jnp.where(top, 1.0 / den, 1.0)
        wide = jnp.broadcast_to(den, (8, EXTRA))
        for a in range(8):
            blk[a, j : j + 1, :D] = val[a : a + 1]
            blk[a, j : j + 1, D:] = wide[a : a + 1]
    for a in range(8):
        blkb[a] = blk[a, :, :D].astype(BF)
    gather(blkb, every, z, y, (gz1, gz2), (gy1, gy2))

    rows = NZ * NY * IM

    def merged(ref, a):
        return ref[a].astype(F32).reshape(rows, D).astype(BF)

    def forward(e, carry):
        xe, ge = merged(every, e), merged(every, 4 + e)
        hidden = mm(xe, win_ref[e], NT)
        act, pull = jax.vjp(jax.nn.gelu, hidden)
        act = act.astype(BF)
        dhid = pull(mm(ge, wout_ref[e], NT))[0].astype(BF)
        act_s[e] = act
        dhid_s[e] = dhid
        outs[e] = mm(act, wout_ref[e]).reshape(NZ * NY, IM, D).astype(BF)
        outs[4 + e] = mm(dhid, win_ref[e]).reshape(NZ * NY, IM, D).astype(BF)
        return carry

    def weight_grads(e, carry):
        gout_ref[e] = mm(act_s[e], merged(every, 4 + e), TN).astype(BF)
        gin_ref[e] = mm(dhid_s[e], merged(every, e), TN).astype(BF)
        return carry

    lax.fori_loop(0, 4, forward, 0)
    scatter(
        outs, total, ring, z_out, z_in, z, y, (sz1, sz2), (sy1, sy2),
        lambda: lax.fori_loop(0, 4, weight_grads, 0),
    )

    lane = lax.broadcasted_iota(jnp.int32, (8, EXTRA), 1)
    for a in range(8):
        val = total[a]
        if a < 4:
            extra = jnp.zeros((8, EXTRA), F32)
        else:
            mean = jnp.sum(blk[a - 4, :, :D] * val, 1, keepdims=True)
            extra = three(mean, lane, 0) + three(1.0 / blk[a - 4, :, D : D + 1], lane, 32)
        for j in range(IM):
            res[j, a : a + 1, :D] = val[j : j + 1]
            res[j, a : a + 1, D:] = extra[j : j + 1]
    for j in range(IM):
        resb[j] = res[j].astype(BF)
    give_back(resb, back, (bq1, bq2), (bj1, bj2))

    slots = back[...].astype(F32).reshape(cols, D + EXTRA).astype(BF)
    slot_rows, extra = slots[:, :D], slots[:, D:]
    which = lax.broadcasted_iota(jnp.int32, (8, EXTRA), 0)
    pick = (lax.broadcasted_iota(jnp.int32, (8, EXTRA), 1) >> 5) == which
    scalars = mm(jnp.where(pick, 1.0, 0.0).astype(BF), extra, NT)
    mean, den_inv = scalars[0:1], scalars[1:2]
    prods = mm(both_b, slot_rows, NT)
    dispatch = expo * den_inv
    taken = combine * prods[m:]
    dot = jnp.sum(jnp.where(first, taken, 0.0), 1, keepdims=True)
    dlog = jnp.where(first, taken - combine * dot, dispatch * (prods[:m] - mean))
    centre = jnp.sum(dlog * logits, 1, keepdims=True)
    pulled = (SCALE * dlog * col_inv).astype(BF)
    grad = mm(jnp.where(first, 0.0, dispatch).astype(BF), slot_rows)
    grad = grad + row_inv * (mm(pulled, params_b, NT) - x * (row_inv * centre))
    xs[...] = jnp.concatenate([grad, grad], 0).T
    low = lax.broadcasted_iota(jnp.int32, (1, 2 * m), 1) < m
    for e in range(NE):
        a, b, c = e * feats, e * feats + feats // 2, (e + 1) * feats
        chunk[e] = jnp.where(low, xs[a:b, :], xs[b:c, :]).astype(BF)
    spread(chunk, y_ref, (s2a, s2b))()


def whole(x, w, win, wout):
    _, feats, lanes = x.shape
    cols = w.shape[1]
    experts, f, d = win.shape
    dma = pltpu.SemaphoreType.DMA
    ring = dma((NZ, NY // 2 + 1, 2))

    def two(*shape):
        return [dma(shape), dma(shape)]

    block = (8, IM, d)
    return pl.pallas_call(
        whole_kernel,
        out_shape=(
            jax.ShapeDtypeStruct((NE, feats // 2, lanes), BF),
            jax.ShapeDtypeStruct(win.shape, BF),
            jax.ShapeDtypeStruct(win.shape, BF),
        ),
        in_specs=[pl.BlockSpec(memory_space=pltpu.VMEM)] * 4,
        out_specs=(pl.BlockSpec(memory_space=pltpu.VMEM),) * 3,
        scratch_shapes=[
            pltpu.VMEM(x.shape, BF),
            pltpu.VMEM((4, 8) + w.shape, BF),
            pltpu.VMEM((d, lanes), F32),
            pltpu.VMEM((d, cols), F32),
            pltpu.VMEM((4, IM, 8, d + EXTRA), BF),
            pltpu.VMEM((4, IM, 8, d + EXTRA), BF),
            pltpu.VMEM((IM, 8, d + EXTRA), BF),
            pltpu.VMEM((IM, 8, d + EXTRA), BF),
            pltpu.VMEM((8, IM, d + EXTRA), F32),
            pltpu.VMEM(block, BF),
            pltpu.VMEM((8, NZ * NY, IM, d), BF),
            pltpu.VMEM((8, NZ * NY, IM, d), BF),
            pltpu.VMEM((experts, NZ * NY * IM, f), BF),
            pltpu.VMEM((experts, NZ * NY * IM, f), BF),
            pltpu.VMEM((NZ, NY // 2, 2) + block, BF),
            pltpu.VMEM((NZ,) + block, BF),
            pltpu.VMEM((NZ,) + block, BF),
            pltpu.VMEM(block, F32),
            pltpu.VMEM((IM, 8, d + EXTRA), F32),
            pltpu.VMEM((IM, 8, d + EXTRA), BF),
            pltpu.VMEM((4, IM, 8, d + EXTRA), BF),
            pltpu.VMEM((NE, feats // 2, lanes), BF),
            *two(NE), *two(4), *two(8), *two(IM, 4), *two(IM), *two(NZ), ring, ring,
            *two(NZ), ring, ring, *two(IM, 4), *two(IM), *two(NE),
        ],
        compiler_params=pltpu.CompilerParams(
            collective_id=0, has_side_effects=True, vmem_limit_bytes=48 * 2**20
        ),
    )(x, w, win, wout)


def local(tokens, slot_params, w_in, w_out, out_grad):
    images, patches, feats = tokens.shape
    m = patches // 4
    slots = slot_params.shape[1]

    def cut(x):
        return jnp.transpose(x.reshape(images, 4, m, feats), (0, 1, 3, 2)).reshape(NE, feats, m)

    packed = jnp.concatenate([cut(tokens), cut(out_grad)], 2)
    params = jnp.transpose(slot_params.reshape(feats, IM, 4, 1, 4), (0, 2, 1, 3, 4))
    params = jnp.broadcast_to(params, (feats, 4, IM, 2, 4)).reshape(feats, 2 * slots)
    grad, grad_w_in, grad_w_out = whole(packed, params, jnp.swapaxes(w_in, 1, 2), w_out)
    grad = jnp.transpose(grad.reshape(images, 4, feats // 2, 2, m), (0, 1, 4, 3, 2))
    return (grad.reshape(images, patches, feats), jnp.swapaxes(grad_w_in, 1, 2), grad_w_out)


def solution(mesh):
    return jax.shard_map(
        local,
        mesh=mesh,
        in_specs=(
            P("dp", None, "expert"),
            P("expert", None),
            P("expert", None, "dp"),
            P("expert", "dp", None),
            P("dp", None, "expert"),
        ),
        out_specs=(P("dp", None, "expert"), P("expert", None, "dp"), P("expert", "dp", None)),
        check_vma=False,
    )
```

```python
import functools

import jax
import jax.numpy as jnp
from jax import lax
from jax.experimental import pallas as pl
from jax.experimental.pallas import tpu as pltpu
from jax.sharding import PartitionSpec as P

SCALE = 32.0
EPS = 1e-06
MESH = pl.DeviceIdType.MESH
BF = jnp.bfloat16
F32 = jnp.float32
NZ, NY = 4, 8
NE = 32
IM = NE // 4
D = 640
EXTRA = 128
NT = (((1,), (1,)), ((), ()))
TN = (((0,), (0,)), ((), ()))


def mm(a, b, dims=(((1,), (0,)), ((), ()))):
    return lax.dot_general(a, b, dims, preferred_element_type=F32)


def at(z, y):
    return lax.rem(z, NZ) * NY + lax.rem(y, NY)


def team(j, q):
    return lax.rem(j, IM) * 4 + lax.rem(q, 4)


def send(src, dst, send_sem, recv_sem, **to):
    copy = pltpu.make_async_remote_copy(
        src_ref=src,
        dst_ref=dst,
        send_sem=send_sem,
        recv_sem=recv_sem,
        device_id=to,
        device_id_type=MESH,
    )
    return copy


def three(x, lane, first):
    hi = x.astype(BF).astype(F32)
    mid = (x - hi).astype(BF).astype(F32)
    low = x - hi - mid
    zero = jnp.zeros_like(x)
    return jnp.where(
        lane == first,
        hi,
        jnp.where(lane == first + 1, mid, jnp.where(lane == first + 2, low, zero)),
    )


def greet(me, z, y):
    barrier = pltpu.get_barrier_semaphore()

    def one(k, carry):
        pl.semaphore_signal(
            barrier, inc=1, device_id={"expert": lax.rem(me + k, NE)}, device_id_type=MESH
        )
        return carry

    lax.fori_loop(1, NE, one, 0)
    others = [at(z, y + 1), at(z, y + NY - 1)] + [at(z + k, y) for k in range(1, NZ)]
    for other in others:
        pl.semaphore_signal(barrier, inc=1, device_id={"dp": other}, device_id_type=MESH)
    return lambda: pl.semaphore_wait(barrier, NE - 1 + len(others))


def spread(x_ref, y_ref, sems):
    me = lax.axis_index("expert")
    hi, lo = lax.div(me, 8), lax.rem(me, 8)
    send_sem, recv_sem = sems

    def copy(dz, k):
        to = lax.rem(hi + dz, 4) * 8 + lax.rem(lo + k, 8)
        at_sem = dz * 8 + k
        return send(
            x_ref.at[to], y_ref.at[me], send_sem.at[at_sem], recv_sem.at[at_sem], expert=to
        )

    def start(dz, k, carry):
        copy(dz, k).start()
        return carry

    def finish(dz, k, carry):
        copy(dz, k).wait()
        return carry

    def finish_all():
        for dz in (0, 1, 3, 2):
            lax.fori_loop(0 if dz else 1, 8, functools.partial(finish, dz), 0)

    for dz in (2, 1, 3, 0):
        lax.fori_loop(0 if dz else 1, 8, functools.partial(start, dz), 0)
    y_ref[me] = x_ref[me]
    return finish_all


def share_along(w_ref, v_ref, sems):
    me = lax.axis_index("expert")
    hi, lo = lax.div(me, 8), lax.rem(me, 8)
    copies = []
    for k in range(1, 4):
        to = lax.rem(hi + k, 4) * 8 + lo
        copies.append(
            send(w_ref, v_ref.at[hi, lo], sems[0].at[k], sems[1].at[k], expert=to)
        )
        copies[-1].start()
    v_ref[hi, lo] = w_ref[...]
    return copies


def share_across(v_ref, sems):
    me = lax.axis_index("expert")
    hi, lo = lax.div(me, 8), lax.rem(me, 8)
    copies = []
    for k in range(1, 8):
        to = hi * 8 + lax.rem(lo + k, 8)
        copies.append(
            send(v_ref.at[:, lo], v_ref.at[:, lo], sems[0].at[k], sems[1].at[k], expert=to)
        )
        copies[-1].start()
    return copies


STEPS = ((2, 0), (2, 1), (1, 0), (3, 0), (1, 1), (3, 1), (0, 1), (0, 0))


def moved(j, dz, dx):
    return lax.rem(lax.div(j, 2) + dz, 4) * 2 + lax.rem(j + dx, 2)


def collect(x_ref, o_ref, part, total, q_sems, j_sems):
    me = lax.axis_index("expert")
    j, q = lax.div(me, 4), lax.rem(me, 4)
    q_copies, j_copies = {}, {}
    for step, (dz, dx) in enumerate(STEPS):
        to = moved(j, dz, dx)
        for k in range(1, 4):
            q_copies[step, k] = send(
                x_ref.at[lax.rem(q + k, 4), to],
                part.at[k, step],
                q_sems[0].at[step, k],
                q_sems[1].at[step, k],
                expert=team(j, q + k),
            )
            q_copies[step, k].start()
    for step, (dz, dx) in enumerate(STEPS):
        to = moved(j, dz, dx)
        for k in range(1, 4):
            q_copies[step, k].wait_recv()
        summed = x_ref[q, to].astype(F32)
        for k in range(1, 4):
            summed = summed + part[k, step].astype(F32)
        if (dz, dx) == (0, 0):
            o_ref[j] = summed.astype(BF)
            continue
        total[step] = summed.astype(BF)
        j_copies[step] = send(
            total.at[step],
            o_ref.at[j],
            j_sems[0].at[step],
            j_sems[1].at[step],
            expert=team(to, q),
        )
        j_copies[step].start()
    for copy in j_copies.values():
        copy.wait()
    for copy in q_copies.values():
        copy.wait_send()


def give_back(x_ref, o_ref, q_sems, j_sems):
    me = lax.axis_index("expert")
    j, q = lax.div(me, 4), lax.rem(me, 4)
    q_copies, j_copies = {}, {}
    for step, (dz, dx) in enumerate(STEPS[:-1]):
        to = moved(j, dz, dx)
        j_copies[step] = send(
            x_ref.at[to],
            o_ref.at[q, j],
            j_sems[0].at[step],
            j_sems[1].at[step],
            expert=team(to, q),
        )
        j_copies[step].start()
    o_ref[q, j] = x_ref[j]
    for step in range(IM - 1, -1, -1):
        dz, dx = STEPS[step]
        here = moved(j, 4 - dz, dx)
        if step in j_copies:
            j_copies[step].wait_recv()
        for k in range(1, 4):
            q_copies[step, k] = send(
                o_ref.at[q, here],
                o_ref.at[q, here],
                q_sems[0].at[step, k],
                q_sems[1].at[step, k],
                expert=team(j, q + k),
            )
            q_copies[step, k].start()
    for copy in q_copies.values():
        copy.wait()
    for copy in j_copies.values():
        copy.wait_send()


ZF = 6
HALF = NY // 2


def ring_rows(step, way, first, count):
    if step < HALF:
        return pl.ds(first, count)
    return pl.ds(first + way * (count // 2), count // 2)


def gather(b_ref, y_ref, z, y, z_sems, y_sems, zb_sems, yb_sems):
    p = at(z, y)

    def y_copy(chain, step, way):
        slot = at(z + chain, y + (NY - (step - 1) if way == 0 else step - 1))
        rows = ring_rows(step, way, 0, ZF)
        src = b_ref if chain == 0 and step == 1 else y_ref.at[:, slot]
        return send(
            src.at[rows],
            y_ref.at[rows, slot],
            y_sems[0].at[chain, step, way],
            y_sems[1].at[chain, step, way],
            dp=at(z, y + (1 if way == 0 else NY - 1)),
        )

    def yb_copy(step, way):
        slot = at(z, y + (NY - (step - 1) if way == 0 else step - 1))
        rows = ring_rows(step, way, ZF, 8 - ZF)
        src = b_ref if step == 1 else y_ref.at[:, slot]
        return send(
            src.at[rows],
            y_ref.at[rows, slot],
            yb_sems[0].at[step, way],
            yb_sems[1].at[step, way],
            dp=at(z, y + (1 if way == 0 else NY - 1)),
        )

    def zb_copy(dy, k):
        rows = pl.ds(ZF, 8 - ZF)
        slot = at(z, y + dy)
        src = b_ref if dy == 0 else y_ref.at[:, slot]
        return send(
            src.at[rows],
            y_ref.at[rows, slot],
            zb_sems[0].at[dy, k],
            zb_sems[1].at[dy, k],
            dp=at(z + k, y),
        )

    y_copies, z_copies, yb_copies, zb_copies = {}, {}, {}, {}

    def ring(chain, step):
        if step > 1:
            for way in (0, 1):
                y_copies[chain, step - 1, way].wait_recv()
        elif chain:
            z_copies[NZ - chain].wait_recv()
        for way in (0, 1):
            y_copies[chain, step, way] = y_copy(chain, step, way)
            y_copies[chain, step, way].start()

    def fan(dy):
        for k in (1, 3, 2):
            zb_copies[dy, k] = zb_copy(dy, k)
            zb_copies[dy, k].start()

    def ring_b(step):
        if step > 1:
            for way in (0, 1):
                yb_copies[step - 1, way].wait_recv()
        if step <= HALF:
            for way in (0, 1):
                yb_copies[step, way] = yb_copy(step, way)
                yb_copies[step, way].start()
        if 1 < step <= HALF:
            fan(step - 1)
            fan(NY - (step - 1))
        elif step > HALF:
            fan(HALF)

    ring_b(1)
    ring(0, 1)
    for k in (3, 1, 2):
        z_copies[k] = send(
            b_ref.at[pl.ds(0, ZF)],
            y_ref.at[pl.ds(0, ZF), p],
            z_sems[0].at[k],
            z_sems[1].at[k],
            dp=at(z + k, y),
        )
        z_copies[k].start()
    fan(0)
    y_ref[:, p] = b_ref[...]
    ring_b(2)
    ring(0, 2)
    ring(1, 1)
    ring(3, 1)
    ring_b(3)
    ring(0, 3)
    ring(2, 1)
    ring(1, 2)
    ring(3, 2)
    ring_b(4)
    ring(0, 4)
    ring(2, 2)
    ring(1, 3)
    ring(3, 3)
    ring_b(5)
    ring(2, 3)
    ring(1, 4)
    ring(3, 4)
    ring(2, 4)
    for chain in (0, 1, 3, 2):
        for way in (0, 1):
            y_copies[chain, HALF, way].wait_recv()
    for copy in zb_copies.values():
        copy.wait()
    for copies in (z_copies, y_copies, yb_copies):
        for copy in copies.values():
            copy.wait_send()


def scatter(
    p_ref, total, ring, z_out, z_in, ring_b, zb_in,
    z, y, z_sems, y_sems, zb_sems, yb_sems, meanwhile,
):
    last = 8 - ZF

    def ahead(step, way):
        return step if way == 0 else NY - step

    def y_copy(chain, step, way):
        slot = at(z + chain, y + ahead(step, way))
        rows = ring_rows(step, way, 0, ZF)
        src = p_ref.at[:, slot] if step == HALF else ring.at[chain, step, way]
        return send(
            src.at[rows],
            ring.at[chain, step - 1, way, rows],
            y_sems[0].at[chain, step, way],
            y_sems[1].at[chain, step, way],
            dp=at(z, y + (1 if way == 0 else NY - 1)),
        )

    def yb_copy(step, way):
        rows = ring_rows(step, way, 0, last)
        return send(
            ring_b.at[step, way, rows],
            ring_b.at[step - 1, way, rows],
            yb_sems[0].at[step, way],
            yb_sems[1].at[step, way],
            dp=at(z, y + (1 if way == 0 else NY - 1)),
        )

    order = (1, 3, 2, 0)
    y_copies, z_copies, yb_copies, zb_copies = {}, {}, {}, {}
    for chain in order:
        for way in (0, 1):
            y_copies[chain, HALF, way] = y_copy(chain, HALF, way)
            y_copies[chain, HALF, way].start()
    for dy in (4, 3, 5, 2, 6, 1, 7, 0):
        for k in (2, 1, 3):
            zb_copies[dy, k] = send(
                p_ref.at[pl.ds(ZF, last), at(z + k, y + dy)],
                zb_in.at[dy, k],
                zb_sems[0].at[dy, k],
                zb_sems[1].at[dy, k],
                dp=at(z + k, y),
            )
            zb_copies[dy, k].start()
    meanwhile()

    def along_z(dy, a):
        here = p_ref[ZF + a, at(z, y + dy)].astype(F32)
        for k in (1, 2, 3):
            here = here + zb_in[dy, k, a].astype(F32)
        return here

    def step_b(step):
        for way in (0, 1):
            dy = ahead(step, way)
            if step < HALF:
                yb_copies[step + 1, way].wait_recv()
            if step < HALF or way == 0:
                for k in (1, 2, 3):
                    zb_copies[dy, k].wait_recv()
            for a in range(last):
                half = a // (last // 2) == way
                if step == HALF and not half:
                    continue
                mine = along_z(dy, a)
                if step < HALF - 1 or (step == HALF - 1 and half):
                    mine = mine + ring_b[step, way, a].astype(F32)
                ring_b[step, way, a] = mine.astype(BF)
            yb_copies[step, way] = yb_copy(step, way)
            yb_copies[step, way].start()

    step_b(HALF)
    for step in range(HALF - 1, 0, -1):
        for chain in order:
            for way in (0, 1):
                y_copies[chain, step + 1, way].wait_recv()
                slot = at(z + chain, y + ahead(step, way))
                for a in range(ZF):
                    mine = p_ref[a, slot]
                    if step < HALF - 1 or a // (ZF // 2) == way:
                        mine = (mine.astype(F32) + ring[chain, step, way, a].astype(F32)).astype(BF)
                    ring[chain, step, way, a] = mine
                y_copies[chain, step, way] = y_copy(chain, step, way)
                y_copies[chain, step, way].start()
        step_b(step)
    for chain in order:
        for way in (0, 1):
            y_copies[chain, 1, way].wait_recv()
        here = at(z + chain, y)
        for a in range(ZF):
            summed = (
                p_ref[a, here].astype(F32)
                + ring[chain, 0, 0, a].astype(F32)
                + ring[chain, 0, 1, a].astype(F32)
            )
            if chain == 0:
                total[a] = summed
            else:
                z_out[chain, a] = summed.astype(BF)
        if chain != 0:
            z_copies[chain] = send(
                z_out.at[chain],
                z_in.at[chain],
                z_sems[0].at[chain],
                z_sems[1].at[chain],
                dp=at(z + chain, y),
            )
            z_copies[chain].start()
    for way in (0, 1):
        yb_copies[1, way].wait_recv()
    for k in (1, 2, 3):
        zb_copies[0, k].wait_recv()
    for a in range(last):
        total[ZF + a] = (
            along_z(0, a) + ring_b[0, 0, a].astype(F32) + ring_b[0, 1, a].astype(F32)
        )
    for chain in (1, 3, 2):
        z_copies[chain].wait_recv()
    for a in range(ZF):
        total[a] = (
            total[a]
            + z_in[1, a].astype(F32)
            + z_in[2, a].astype(F32)
            + z_in[3, a].astype(F32)
        )
    for copies in (z_copies, y_copies, yb_copies, zb_copies):
        for copy in copies.values():
            copy.wait_send()


def whole_kernel(
    t_hbm, g_hbm, w_hbm, win_hbm, wout_hbm,
    y_ref, gin_ref, gout_ref,
    t_ref, g_ref, w_ref, wide, wide_g, x_in, w_in, win_ref, wout_ref, y_in,
    xin, vin, xs, ps, parts, part, part_sum, sums, blk, blkb, every, outs, act_s, dhid_s,
    ring, z_out, z_in, ring_b, zb_in, total, res, resb, back, chunk,
    wsem, s1a, s1b, sa1, sa2, sb1, sb2, cq1, cq2, cj1, cj2, gz1, gz2, gy1, gy2, gzb1, gzb2, gyb1, gyb2,
    sz1, sz2, sy1, sy2, szb1, szb2, syb1, syb2, bq1, bq2, bj1, bj2, s2a, s2b,
):
    me = lax.axis_index("expert")
    quarter = lax.rem(me, 4)
    p = lax.axis_index("dp")
    z, y = lax.div(p, NY), lax.rem(p, NY)
    all_here = greet(me, z, y)
    pairs = (
        (t_hbm, t_ref), (g_hbm, g_ref), (w_hbm, w_ref), (win_hbm, win_ref), (wout_hbm, wout_ref)
    )
    loads = [
        pltpu.make_async_copy(src, dst, wsem.at[i]) for i, (src, dst) in enumerate(pairs)
    ]
    for load in loads:
        load.start()
    for load in loads[:3]:
        load.wait()

    feats = t_ref.shape[0]
    for h in (0, 1):
        lanes = slice(128 * h, 128 * h + 128)
        wide[h] = t_ref[:, :, lanes].astype(F32).reshape(wide.shape[1:])
        wide_g[h] = g_ref[:, :, lanes].astype(F32).reshape(wide.shape[1:])
    left = lax.broadcasted_iota(jnp.int32, (1, 128), 1) < 64
    for j in range(IM):
        for h in (0, 1):
            t = wide[h, pl.ds(j, feats, IM), :]
            g = wide_g[h, pl.ds(j, feats, IM), :]
            x_in[4 * j + 2 * h] = jnp.where(left, t, pltpu.roll(g, 64, 1)).astype(BF)
            x_in[4 * j + 2 * h + 1] = jnp.where(left, pltpu.roll(t, 64, 1), g).astype(BF)
    slots = w_ref.shape[1]
    col = lax.broadcasted_iota(jnp.int32, (slots, 2 * slots), 1)
    slot = ((col >> 3) & 7) * 16 + (col >> 6) * 4 + (col & 3)
    pick = lax.broadcasted_iota(jnp.int32, (slots, 2 * slots), 0) == slot
    w_in[...] = mm(w_ref[...], jnp.where(pick, 1.0, 0.0).astype(BF)).astype(BF)
    all_here()

    along = share_along(w_in, vin, (sa1, sa2))
    finish = spread(x_in, xin, (s1a, s1b))
    for copy in along:
        copy.wait()
    across = share_across(vin, (sb1, sb2))
    finish()
    for e in range(NE):
        xs[e * feats : (e + 1) * feats, :] = xin[e].astype(F32)
    both = xs[...].T
    both_b = both.astype(BF)
    m = both.shape[0] // 2
    for copy in across:
        copy.wait()
    for e in range(NE):
        ps[e * feats : (e + 1) * feats, :] = vin[e // 8, e % 8].astype(F32)
    params = ps[...]
    params_b = params.astype(BF)

    cols = 2 * NE * 4
    first = (lax.broadcasted_iota(jnp.int32, (1, cols), 1) & 4) == 0
    x = both[:m]
    row_inv = lax.rsqrt(jnp.sum(x * x, 1, keepdims=True) + EPS)
    col_inv = lax.rsqrt(jnp.sum(params * params, 0, keepdims=True) + EPS)
    logits = SCALE * mm(both_b[:m], params_b) * row_inv * col_inv
    expo = jnp.exp(logits)
    combine = expo / (0.5 * jnp.sum(expo, 1, keepdims=True))
    weights = jnp.concatenate([jnp.where(first, expo, 0.0), jnp.where(first, 0.0, combine)], 0).T
    slot_part = mm(weights.astype(BF), both_b)
    lane = lax.broadcasted_iota(jnp.int32, (cols, EXTRA), 1)
    upper = (lax.broadcasted_iota(jnp.int32, (cols, 1), 0) & 4) == 0
    den = jnp.where(upper, jnp.sum(weights, 1, keepdims=True), 0.0)
    den = three(den, lane, 32 * quarter)
    for e in range(NE):
        rows = slice(8 * e, 8 * e + 8)
        parts[e // IM, e % IM, :, :D] = slot_part[rows].astype(BF)
        parts[e // IM, e % IM, :, D:] = den[rows].astype(BF)
    collect(parts, sums, part, part_sum, (cq1, cq2), (cj1, cj2))

    top = lax.broadcasted_iota(jnp.int32, (8, 1), 0) < 4
    for j in range(IM):
        val = sums[j, :, :D].astype(F32)
        den = jnp.sum(sums[j, :, D:].astype(F32), 1, keepdims=True)
        val = val * jnp.where(top, 1.0 / den, 1.0)
        den_wide = jnp.broadcast_to(den, (8, EXTRA))
        for a in range(8):
            blk[a, j : j + 1, :D] = val[a : a + 1]
            blk[a, j : j + 1, D:] = den_wide[a : a + 1]
    for a in range(8):
        blkb[a] = blk[a, :, :D].astype(BF)
    gather(blkb, every, z, y, (gz1, gz2), (gy1, gy2), (gzb1, gzb2), (gyb1, gyb2))
    for load in loads[3:]:
        load.wait()

    rows = NZ * NY * IM

    def merged(ref, a):
        return ref[a].astype(F32).reshape(rows, D).astype(BF)

    def forward(e, carry):
        xe, ge = merged(every, e), merged(every, 4 + e)
        hidden = mm(xe, win_ref[e], NT)
        act, pull = jax.vjp(jax.nn.gelu, hidden)
        act = act.astype(BF)
        dhid = pull(mm(ge, wout_ref[e], NT))[0].astype(BF)
        act_s[e] = act
        dhid_s[e] = dhid
        outs[e] = mm(act, wout_ref[e]).reshape(NZ * NY, IM, D).astype(BF)
        outs[4 + e] = mm(dhid, win_ref[e]).reshape(NZ * NY, IM, D).astype(BF)
        return carry

    def weight_grads(e, carry):
        gout_ref[e] = mm(act_s[e], merged(every, 4 + e), TN).astype(BF)
        gin_ref[e] = mm(dhid_s[e], merged(every, e), TN).astype(BF)
        return carry

    lax.fori_loop(0, 4, forward, 0)
    scatter(
        outs, total, ring, z_out, z_in, ring_b, zb_in, z, y,
        (sz1, sz2), (sy1, sy2), (szb1, szb2), (syb1, syb2),
        lambda: lax.fori_loop(0, 4, weight_grads, 0),
    )

    lane = lax.broadcasted_iota(jnp.int32, (8, EXTRA), 1)
    for a in range(8):
        val = total[a]
        if a < 4:
            extra = jnp.zeros((8, EXTRA), F32)
        else:
            mean = jnp.sum(blk[a - 4, :, :D] * val, 1, keepdims=True)
            extra = three(mean, lane, 0) + three(1.0 / blk[a - 4, :, D : D + 1], lane, 32)
        for j in range(IM):
            res[j, a : a + 1, :D] = val[j : j + 1]
            res[j, a : a + 1, D:] = extra[j : j + 1]
    for j in range(IM):
        resb[j] = res[j].astype(BF)
    give_back(resb, back, (bq1, bq2), (bj1, bj2))

    slots = back[...].astype(F32).reshape(cols, D + EXTRA).astype(BF)
    slot_rows, extra = slots[:, :D], slots[:, D:]
    which = lax.broadcasted_iota(jnp.int32, (8, EXTRA), 0)
    pick = (lax.broadcasted_iota(jnp.int32, (8, EXTRA), 1) >> 5) == which
    scalars = mm(jnp.where(pick, 1.0, 0.0).astype(BF), extra, NT)
    mean, den_inv = scalars[0:1], scalars[1:2]
    prods = mm(both_b, slot_rows, NT)
    dispatch = expo * den_inv
    taken = combine * prods[m:]
    dot = jnp.sum(jnp.where(first, taken, 0.0), 1, keepdims=True)
    dlog = jnp.where(first, taken - combine * dot, dispatch * (prods[:m] - mean))
    centre = jnp.sum(dlog * logits, 1, keepdims=True)
    pulled = (SCALE * dlog * col_inv).astype(BF)
    grad = mm(jnp.where(first, 0.0, dispatch).astype(BF), slot_rows)
    grad = grad + row_inv * (mm(pulled, params_b, NT) - x * (row_inv * centre))
    xs[...] = jnp.concatenate([grad, grad], 0).T
    low = lax.broadcasted_iota(jnp.int32, (1, 2 * m), 1) < m
    for e in range(NE):
        a, b, c = e * feats, e * feats + feats // 2, (e + 1) * feats
        chunk[e] = jnp.where(low, xs[a:b, :], xs[b:c, :]).astype(BF)
    spread(chunk, y_in, (s2a, s2b))()
    for j in range(IM):
        for h in (0, 1):
            a, b = y_in[4 * j + 2 * h].astype(F32), y_in[4 * j + 2 * h + 1].astype(F32)
            wide[h, pl.ds(j, feats // 2, IM), :] = jnp.where(left, a, pltpu.roll(b, 64, 1))
            wide[h, pl.ds(IM * (feats // 2) + j, feats // 2, IM), :] = jnp.where(
                left, pltpu.roll(a, 64, 1), b
            )
    for h in (0, 1):
        lanes = slice(128 * h, 128 * h + 128)
        y_ref[:, :, lanes] = wide[h].reshape(feats, IM, 128).astype(BF)


def whole(t, g, w, win, wout):
    feats, _, patches = t.shape
    lanes = patches // 2
    slots = w.shape[1]
    cols = 2 * slots
    experts, f, d = win.shape
    dma = pltpu.SemaphoreType.DMA
    ring = dma((NZ, HALF + 1, 2))
    last = 8 - ZF

    def two(*shape):
        return [dma(shape), dma(shape)]

    block = (8, IM, d)
    vmem = pl.BlockSpec(memory_space=pltpu.VMEM)
    hbm = pl.BlockSpec(memory_space=pl.ANY)
    return pl.pallas_call(
        whole_kernel,
        out_shape=(
            jax.ShapeDtypeStruct(t.shape, BF),
            jax.ShapeDtypeStruct(win.shape, BF),
            jax.ShapeDtypeStruct(win.shape, BF),
        ),
        in_specs=[hbm] * 5,
        out_specs=(vmem,) * 3,
        scratch_shapes=[
            pltpu.VMEM(t.shape, BF),
            pltpu.VMEM(t.shape, BF),
            pltpu.VMEM(w.shape, BF),
            pltpu.VMEM((2, feats * IM, lanes), F32),
            pltpu.VMEM((2, feats * IM, lanes), F32),
            pltpu.VMEM((NE, feats, lanes), BF),
            pltpu.VMEM((feats, cols), BF),
            pltpu.VMEM(win.shape, BF),
            pltpu.VMEM(win.shape, BF),
            pltpu.VMEM((NE, feats // 2, lanes), BF),
            pltpu.VMEM((NE, feats, lanes), BF),
            pltpu.VMEM((4, 8, feats, cols), BF),
            pltpu.VMEM((d, lanes), F32),
            pltpu.VMEM((d, cols), F32),
            pltpu.VMEM((4, IM, 8, d + EXTRA), BF),
            pltpu.VMEM((4, IM, 8, d + EXTRA), BF),
            pltpu.VMEM((IM, 8, d + EXTRA), BF),
            pltpu.VMEM((IM, 8, d + EXTRA), BF),
            pltpu.VMEM((8, IM, d + EXTRA), F32),
            pltpu.VMEM(block, BF),
            pltpu.VMEM((8, NZ * NY, IM, d), BF),
            pltpu.VMEM((8, NZ * NY, IM, d), BF),
            pltpu.VMEM((experts, NZ * NY * IM, f), BF),
            pltpu.VMEM((experts, NZ * NY * IM, f), BF),
            pltpu.VMEM((NZ, HALF, 2, ZF, IM, d), BF),
            pltpu.VMEM((NZ, ZF, IM, d), BF),
            pltpu.VMEM((NZ, ZF, IM, d), BF),
            pltpu.VMEM((HALF + 1, 2, last, IM, d), BF),
            pltpu.VMEM((NY, NZ, last, IM, d), BF),
            pltpu.VMEM(block, F32),
            pltpu.VMEM((IM, 8, d + EXTRA), F32),
            pltpu.VMEM((IM, 8, d + EXTRA), BF),
            pltpu.VMEM((4, IM, 8, d + EXTRA), BF),
            pltpu.VMEM((NE, feats // 2, lanes), BF),
            dma((5,)), *two(NE), *two(4), *two(8), *two(IM, 4), *two(IM),
            *two(NZ), ring, ring, *two(NY, NZ), *two(HALF + 1, 2),
            *two(NZ), ring, ring, *two(NY, NZ), *two(HALF + 1, 2),
            *two(IM, 4), *two(IM), *two(NE),
        ],
        compiler_params=pltpu.CompilerParams(
            collective_id=0, has_side_effects=True, vmem_limit_bytes=52 * 2**20
        ),
    )(t, g, w, win, wout)


def local(tokens, slot_params, w_in, w_out, out_grad):
    grad, grad_w_in, grad_w_out = whole(
        jnp.transpose(tokens, (2, 0, 1)),
        jnp.transpose(out_grad, (2, 0, 1)),
        slot_params,
        jnp.swapaxes(w_in, 1, 2),
        w_out,
    )
    return (jnp.transpose(grad, (1, 2, 0)), jnp.swapaxes(grad_w_in, 1, 2), grad_w_out)


def solution(mesh):
    return jax.shard_map(
        local,
        mesh=mesh,
        in_specs=(
            P("dp", None, "expert"),
            P("expert", None),
            P("expert", None, "dp"),
            P("expert", "dp", None),
            P("dp", None, "expert"),
        ),
        out_specs=(P("dp", None, "expert"), P("expert", None, "dp"), P("expert", "dp", None)),
        check_vma=False,
    )
```

```python
import functools

import jax
import jax.numpy as jnp
from jax import lax
from jax.experimental import pallas as pl
from jax.experimental.pallas import tpu as pltpu
from jax.sharding import PartitionSpec as P

SCALE = 32.0
EPS = 1e-06
MESH = pl.DeviceIdType.MESH
BF = jnp.bfloat16
F32 = jnp.float32
NZ, NY = 4, 8
NE = 32
IM = NE // 4
D = 640
EXTRA = 128
NT = (((1,), (1,)), ((), ()))
TN = (((0,), (0,)), ((), ()))


def mm(a, b, dims=(((1,), (0,)), ((), ()))):
    return lax.dot_general(a, b, dims, preferred_element_type=F32)


def at(z, y):
    return lax.rem(z, NZ) * NY + lax.rem(y, NY)


def team(j, q):
    return lax.rem(j, IM) * 4 + lax.rem(q, 4)


def send(src, dst, send_sem, recv_sem, **to):
    copy = pltpu.make_async_remote_copy(
        src_ref=src,
        dst_ref=dst,
        send_sem=send_sem,
        recv_sem=recv_sem,
        device_id=to,
        device_id_type=MESH,
    )
    return copy


def three(x, lane, first):
    hi = x.astype(BF).astype(F32)
    mid = (x - hi).astype(BF).astype(F32)
    low = x - hi - mid
    zero = jnp.zeros_like(x)
    return jnp.where(
        lane == first,
        hi,
        jnp.where(lane == first + 1, mid, jnp.where(lane == first + 2, low, zero)),
    )


def greet(me, z, y):
    barrier = pltpu.get_barrier_semaphore()

    def one(k, carry):
        pl.semaphore_signal(
            barrier, inc=1, device_id={"expert": lax.rem(me + k, NE)}, device_id_type=MESH
        )
        return carry

    lax.fori_loop(1, NE, one, 0)
    others = [at(z, y + 1), at(z, y + NY - 1)] + [at(z + k, y) for k in range(1, NZ)]
    for other in others:
        pl.semaphore_signal(barrier, inc=1, device_id={"dp": other}, device_id_type=MESH)
    return lambda: pl.semaphore_wait(barrier, NE - 1 + len(others))


def spread(x_ref, y_ref, sems):
    me = lax.axis_index("expert")
    hi, lo = lax.div(me, 8), lax.rem(me, 8)
    send_sem, recv_sem = sems

    def copy(dz, k):
        to = lax.rem(hi + dz, 4) * 8 + lax.rem(lo + k, 8)
        at_sem = dz * 8 + k
        return send(
            x_ref.at[to], y_ref.at[me], send_sem.at[at_sem], recv_sem.at[at_sem], expert=to
        )

    def start(dz, k, carry):
        copy(dz, k).start()
        return carry

    def finish(dz, k, carry):
        copy(dz, k).wait()
        return carry

    def finish_all():
        for dz in (0, 1, 3, 2):
            lax.fori_loop(0 if dz else 1, 8, functools.partial(finish, dz), 0)

    for dz in (2, 1, 3, 0):
        lax.fori_loop(0 if dz else 1, 8, functools.partial(start, dz), 0)
    y_ref[me] = x_ref[me]
    return finish_all


def share_along(w_ref, v_ref, sems):
    me = lax.axis_index("expert")
    hi, lo = lax.div(me, 8), lax.rem(me, 8)
    copies = []
    for k in range(1, 4):
        to = lax.rem(hi + k, 4) * 8 + lo
        copies.append(
            send(w_ref, v_ref.at[hi, lo], sems[0].at[k], sems[1].at[k], expert=to)
        )
        copies[-1].start()
    v_ref[hi, lo] = w_ref[...]
    return copies


def share_across(v_ref, sems):
    me = lax.axis_index("expert")
    hi, lo = lax.div(me, 8), lax.rem(me, 8)
    copies = []
    for k in range(1, 8):
        to = hi * 8 + lax.rem(lo + k, 8)
        copies.append(
            send(v_ref.at[:, lo], v_ref.at[:, lo], sems[0].at[k], sems[1].at[k], expert=to)
        )
        copies[-1].start()
    return copies


STEPS = ((2, 0), (2, 1), (1, 0), (3, 0), (1, 1), (3, 1), (0, 1), (0, 0))


def moved(j, dz, dx):
    return lax.rem(lax.div(j, 2) + dz, 4) * 2 + lax.rem(j + dx, 2)


def collect(x_ref, o_ref, part, total, q_sems, j_sems):
    me = lax.axis_index("expert")
    j, q = lax.div(me, 4), lax.rem(me, 4)
    q_copies, j_copies = {}, {}
    for step, (dz, dx) in enumerate(STEPS):
        to = moved(j, dz, dx)
        for k in range(1, 4):
            q_copies[step, k] = send(
                x_ref.at[lax.rem(q + k, 4), to],
                part.at[k, step],
                q_sems[0].at[step, k],
                q_sems[1].at[step, k],
                expert=team(j, q + k),
            )
            q_copies[step, k].start()
    for step, (dz, dx) in enumerate(STEPS):
        to = moved(j, dz, dx)
        for k in range(1, 4):
            q_copies[step, k].wait_recv()
        summed = x_ref[q, to].astype(F32)
        for k in range(1, 4):
            summed = summed + part[k, step].astype(F32)
        if (dz, dx) == (0, 0):
            o_ref[j] = summed.astype(BF)
            continue
        total[step] = summed.astype(BF)
        j_copies[step] = send(
            total.at[step],
            o_ref.at[j],
            j_sems[0].at[step],
            j_sems[1].at[step],
            expert=team(to, q),
        )
        j_copies[step].start()
    for copy in j_copies.values():
        copy.wait()
    for copy in q_copies.values():
        copy.wait_send()


def give_back(x_ref, o_ref, q_sems, j_sems):
    me = lax.axis_index("expert")
    j, q = lax.div(me, 4), lax.rem(me, 4)
    q_copies, j_copies = {}, {}
    for step, (dz, dx) in enumerate(STEPS[:-1]):
        to = moved(j, dz, dx)
        j_copies[step] = send(
            x_ref.at[to],
            o_ref.at[q, j],
            j_sems[0].at[step],
            j_sems[1].at[step],
            expert=team(to, q),
        )
        j_copies[step].start()
    o_ref[q, j] = x_ref[j]
    for step in range(IM - 1, -1, -1):
        dz, dx = STEPS[step]
        here = moved(j, 4 - dz, dx)
        if step in j_copies:
            j_copies[step].wait_recv()
        for k in range(1, 4):
            q_copies[step, k] = send(
                o_ref.at[q, here],
                o_ref.at[q, here],
                q_sems[0].at[step, k],
                q_sems[1].at[step, k],
                expert=team(j, q + k),
            )
            q_copies[step, k].start()
    for copy in q_copies.values():
        copy.wait()
    for copy in j_copies.values():
        copy.wait_send()


ZF = 6
HALF = NY // 2


def ring_rows(step, way, first, count):
    if step < HALF:
        return pl.ds(first, count)
    return pl.ds(first + way * (count // 2), count // 2)


def gather(b_ref, y_ref, z, y, z_sems, y_sems, zb_sems, yb_sems):
    p = at(z, y)

    def y_copy(chain, step, way):
        slot = at(z + chain, y + (NY - (step - 1) if way == 0 else step - 1))
        rows = ring_rows(step, way, 0, ZF)
        src = b_ref if chain == 0 and step == 1 else y_ref.at[:, slot]
        return send(
            src.at[rows],
            y_ref.at[rows, slot],
            y_sems[0].at[chain, step, way],
            y_sems[1].at[chain, step, way],
            dp=at(z, y + (1 if way == 0 else NY - 1)),
        )

    def yb_copy(step, way):
        slot = at(z, y + (NY - (step - 1) if way == 0 else step - 1))
        rows = ring_rows(step, way, ZF, 8 - ZF)
        src = b_ref if step == 1 else y_ref.at[:, slot]
        return send(
            src.at[rows],
            y_ref.at[rows, slot],
            yb_sems[0].at[step, way],
            yb_sems[1].at[step, way],
            dp=at(z, y + (1 if way == 0 else NY - 1)),
        )

    def zb_copy(dy, k):
        rows = pl.ds(ZF, 8 - ZF)
        slot = at(z, y + dy)
        src = b_ref if dy == 0 else y_ref.at[:, slot]
        return send(
            src.at[rows],
            y_ref.at[rows, slot],
            zb_sems[0].at[dy, k],
            zb_sems[1].at[dy, k],
            dp=at(z + k, y),
        )

    y_copies, z_copies, yb_copies, zb_copies = {}, {}, {}, {}

    def ring(chain, step):
        if step > 1:
            for way in (0, 1):
                y_copies[chain, step - 1, way].wait_recv()
        elif chain:
            z_copies[NZ - chain].wait_recv()
        for way in (0, 1):
            y_copies[chain, step, way] = y_copy(chain, step, way)
            y_copies[chain, step, way].start()

    def fan(dy):
        for k in (1, 3, 2):
            zb_copies[dy, k] = zb_copy(dy, k)
            zb_copies[dy, k].start()

    def ring_b(step):
        if step > 1:
            for way in (0, 1):
                yb_copies[step - 1, way].wait_recv()
        if step <= HALF:
            for way in (0, 1):
                yb_copies[step, way] = yb_copy(step, way)
                yb_copies[step, way].start()

    ring_b(1)
    ring(0, 1)
    for k in (3, 1, 2):
        z_copies[k] = send(
            b_ref.at[pl.ds(0, ZF)],
            y_ref.at[pl.ds(0, ZF), p],
            z_sems[0].at[k],
            z_sems[1].at[k],
            dp=at(z + k, y),
        )
        z_copies[k].start()
    y_ref[:, p] = b_ref[...]
    ring_b(2)
    ring(0, 2)
    ring(1, 1)
    ring(3, 1)
    fan(0)
    ring_b(3)
    ring(0, 3)
    ring(2, 1)
    fan(1)
    fan(7)
    ring(1, 2)
    ring(3, 2)
    ring_b(4)
    fan(2)
    fan(6)
    ring(0, 4)
    ring(2, 2)
    ring(1, 3)
    ring(3, 3)
    ring_b(5)
    fan(3)
    fan(5)
    fan(4)
    ring(2, 3)
    ring(1, 4)
    ring(3, 4)
    ring(2, 4)
    for chain in (0, 1, 3, 2):
        for way in (0, 1):
            y_copies[chain, HALF, way].wait_recv()
    for copy in zb_copies.values():
        copy.wait()
    for copies in (z_copies, y_copies, yb_copies):
        for copy in copies.values():
            copy.wait_send()


def scatter(
    p_ref, total, ring, z_out, z_in, ring_b, zb_in,
    z, y, z_sems, y_sems, zb_sems, yb_sems,
):
    last = 8 - ZF

    def ahead(step, way):
        return step if way == 0 else NY - step

    def y_copy(chain, step, way):
        slot = at(z + chain, y + ahead(step, way))
        rows = ring_rows(step, way, 0, ZF)
        src = p_ref.at[:, slot] if step == HALF else ring.at[chain, step, way]
        return send(
            src.at[rows],
            ring.at[chain, step - 1, way, rows],
            y_sems[0].at[chain, step, way],
            y_sems[1].at[chain, step, way],
            dp=at(z, y + (1 if way == 0 else NY - 1)),
        )

    def yb_copy(step, way):
        rows = ring_rows(step, way, 0, last)
        return send(
            ring_b.at[step, way, rows],
            ring_b.at[step - 1, way, rows],
            yb_sems[0].at[step, way],
            yb_sems[1].at[step, way],
            dp=at(z, y + (1 if way == 0 else NY - 1)),
        )

    order = (1, 3, 2, 0)
    y_copies, z_copies, yb_copies, zb_copies = {}, {}, {}, {}
    for chain in order:
        for way in (0, 1):
            y_copies[chain, HALF, way] = y_copy(chain, HALF, way)
            y_copies[chain, HALF, way].start()
    for dy in (4, 3, 5, 2, 6, 1, 7, 0):
        for k in (2, 1, 3):
            zb_copies[dy, k] = send(
                p_ref.at[pl.ds(ZF, last), at(z + k, y + dy)],
                zb_in.at[dy, k],
                zb_sems[0].at[dy, k],
                zb_sems[1].at[dy, k],
                dp=at(z + k, y),
            )
            zb_copies[dy, k].start()

    def along_z(dy, a):
        here = p_ref[ZF + a, at(z, y + dy)].astype(F32)
        for k in (1, 2, 3):
            here = here + zb_in[dy, k, a].astype(F32)
        return here

    def step_b(step):
        for way in (0, 1):
            dy = ahead(step, way)
            if step < HALF:
                yb_copies[step + 1, way].wait_recv()
            if step < HALF or way == 0:
                for k in (1, 2, 3):
                    zb_copies[dy, k].wait_recv()
            for a in range(last):
                half = a // (last // 2) == way
                if step == HALF and not half:
                    continue
                mine = along_z(dy, a)
                if step < HALF - 1 or (step == HALF - 1 and half):
                    mine = mine + ring_b[step, way, a].astype(F32)
                ring_b[step, way, a] = mine.astype(BF)
            yb_copies[step, way] = yb_copy(step, way)
            yb_copies[step, way].start()

    step_b(HALF)
    for step in range(HALF - 1, 0, -1):
        for chain in order:
            for way in (0, 1):
                y_copies[chain, step + 1, way].wait_recv()
                slot = at(z + chain, y + ahead(step, way))
                for a in range(ZF):
                    mine = p_ref[a, slot]
                    if step < HALF - 1 or a // (ZF // 2) == way:
                        mine = (mine.astype(F32) + ring[chain, step, way, a].astype(F32)).astype(BF)
                    ring[chain, step, way, a] = mine
                y_copies[chain, step, way] = y_copy(chain, step, way)
                y_copies[chain, step, way].start()
        step_b(step)
    for chain in order:
        for way in (0, 1):
            y_copies[chain, 1, way].wait_recv()
        here = at(z + chain, y)
        for a in range(ZF):
            summed = (
                p_ref[a, here].astype(F32)
                + ring[chain, 0, 0, a].astype(F32)
                + ring[chain, 0, 1, a].astype(F32)
            )
            if chain == 0:
                total[a] = summed
            else:
                z_out[chain, a] = summed.astype(BF)
        if chain != 0:
            z_copies[chain] = send(
                z_out.at[chain],
                z_in.at[chain],
                z_sems[0].at[chain],
                z_sems[1].at[chain],
                dp=at(z + chain, y),
            )
            z_copies[chain].start()
    for way in (0, 1):
        yb_copies[1, way].wait_recv()
    for k in (1, 2, 3):
        zb_copies[0, k].wait_recv()
    for a in range(last):
        total[ZF + a] = (
            along_z(0, a) + ring_b[0, 0, a].astype(F32) + ring_b[0, 1, a].astype(F32)
        )
    for chain in (1, 3, 2):
        z_copies[chain].wait_recv()
    for a in range(ZF):
        total[a] = (
            total[a]
            + z_in[1, a].astype(F32)
            + z_in[2, a].astype(F32)
            + z_in[3, a].astype(F32)
        )
    for copies in (z_copies, y_copies, yb_copies, zb_copies):
        for copy in copies.values():
            copy.wait_send()


def whole_kernel(
    tgw_ref, win_hbm, wout_hbm,
    y_ref, gin_ref, gout_ref,
    wide, wide_g, wide_w, x_in, w_in, win_ref, wout_ref, y_in,
    xin, vin, xs, ps, parts, part, part_sum, sums, blk, blkb, every, outs, act_s, dhid_s,
    ring, z_out, z_in, ring_b, zb_in, total, res, resb, back, chunk,
    wsem, s1a, s1b, sa1, sa2, sb1, sb2, cq1, cq2, cj1, cj2, gz1, gz2, gy1, gy2, gzb1, gzb2, gyb1, gyb2,
    sz1, sz2, sy1, sy2, szb1, szb2, syb1, syb2, bq1, bq2, bj1, bj2, s2a, s2b,
):
    me = lax.axis_index("expert")
    quarter = lax.rem(me, 4)
    p = lax.axis_index("dp")
    z, y = lax.div(p, NY), lax.rem(p, NY)
    all_here = greet(me, z, y)
    pairs = ((win_hbm, win_ref), (wout_hbm, wout_ref))
    loads = [
        pltpu.make_async_copy(src, dst, wsem.at[i]) for i, (src, dst) in enumerate(pairs)
    ]
    for load in loads:
        load.start()

    feats = tgw_ref.shape[0]
    for h in (0, 1):
        lanes = slice(128 * h, 128 * h + 128)
        wide[h] = tgw_ref[:, :IM, lanes].astype(F32).reshape(wide.shape[1:])
        wide_g[h] = tgw_ref[:, IM : 2 * IM, lanes].astype(F32).reshape(wide.shape[1:])
    left = lax.broadcasted_iota(jnp.int32, (1, 128), 1) < 64
    for j in range(IM):
        for h in (0, 1):
            t = wide[h, pl.ds(j, feats, IM), :]
            g = wide_g[h, pl.ds(j, feats, IM), :]
            x_in[4 * j + 2 * h] = jnp.where(left, t, pltpu.roll(g, 64, 1)).astype(BF)
            x_in[4 * j + 2 * h + 1] = jnp.where(left, pltpu.roll(t, 64, 1), g).astype(BF)
    slots = 128
    wide_w[...] = tgw_ref[:, 2 * IM :, :slots].astype(F32).reshape(wide_w.shape)
    w = wide_w[pl.ds(0, feats, IM), :].astype(BF)
    col = lax.broadcasted_iota(jnp.int32, (slots, 2 * slots), 1)
    slot = ((col >> 3) & 7) * 16 + (col >> 6) * 4 + (col & 3)
    pick = lax.broadcasted_iota(jnp.int32, (slots, 2 * slots), 0) == slot
    w_in[...] = mm(w, jnp.where(pick, 1.0, 0.0).astype(BF)).astype(BF)
    all_here()

    along = share_along(w_in, vin, (sa1, sa2))
    finish = spread(x_in, xin, (s1a, s1b))
    for copy in along:
        copy.wait()
    across = share_across(vin, (sb1, sb2))
    finish()
    for e in range(NE):
        xs[e * feats : (e + 1) * feats, :] = xin[e].astype(F32)
    both = xs[...].T
    both_b = both.astype(BF)
    m = both.shape[0] // 2
    for copy in across:
        copy.wait()
    for e in range(NE):
        ps[e * feats : (e + 1) * feats, :] = vin[e // 8, e % 8].astype(F32)
    params = ps[...]
    params_b = params.astype(BF)

    cols = 2 * NE * 4
    first = (lax.broadcasted_iota(jnp.int32, (1, cols), 1) & 4) == 0
    x = both[:m]
    row_inv = lax.rsqrt(jnp.sum(x * x, 1, keepdims=True) + EPS)
    col_inv = lax.rsqrt(jnp.sum(params * params, 0, keepdims=True) + EPS)
    logits = SCALE * mm(both_b[:m], params_b) * row_inv * col_inv
    expo = jnp.exp(logits)
    combine = expo / (0.5 * jnp.sum(expo, 1, keepdims=True))
    weights = jnp.concatenate([jnp.where(first, expo, 0.0), jnp.where(first, 0.0, combine)], 0).T
    slot_part = mm(weights.astype(BF), both_b)
    lane = lax.broadcasted_iota(jnp.int32, (cols, EXTRA), 1)
    upper = (lax.broadcasted_iota(jnp.int32, (cols, 1), 0) & 4) == 0
    den = jnp.where(upper, jnp.sum(weights, 1, keepdims=True), 0.0)
    den = three(den, lane, 32 * quarter)
    for e in range(NE):
        rows = slice(8 * e, 8 * e + 8)
        parts[e // IM, e % IM, :, :D] = slot_part[rows].astype(BF)
        parts[e // IM, e % IM, :, D:] = den[rows].astype(BF)
    collect(parts, sums, part, part_sum, (cq1, cq2), (cj1, cj2))

    top = lax.broadcasted_iota(jnp.int32, (8, 1), 0) < 4
    for j in range(IM):
        val = sums[j, :, :D].astype(F32)
        den = jnp.sum(sums[j, :, D:].astype(F32), 1, keepdims=True)
        val = val * jnp.where(top, 1.0 / den, 1.0)
        den_wide = jnp.broadcast_to(den, (8, EXTRA))
        for a in range(8):
            blk[a, j : j + 1, :D] = val[a : a + 1]
            blk[a, j : j + 1, D:] = den_wide[a : a + 1]
    for a in range(8):
        blkb[a] = blk[a, :, :D].astype(BF)
    gather(blkb, every, z, y, (gz1, gz2), (gy1, gy2), (gzb1, gzb2), (gyb1, gyb2))
    for load in loads:
        load.wait()

    rows = NZ * NY * IM

    def merged(ref, a):
        return ref[a].astype(F32).reshape(rows, D).astype(BF)

    def forward(e, carry):
        xe, ge = merged(every, e), merged(every, 4 + e)
        hidden = mm(xe, win_ref[e], NT)
        act, pull = jax.vjp(jax.nn.gelu, hidden)
        act = act.astype(BF)
        dhid = pull(mm(ge, wout_ref[e], NT))[0].astype(BF)
        act_s[e] = act
        dhid_s[e] = dhid
        outs[e] = mm(act, wout_ref[e]).reshape(NZ * NY, IM, D).astype(BF)
        outs[4 + e] = mm(dhid, win_ref[e]).reshape(NZ * NY, IM, D).astype(BF)
        return carry

    def weight_grads(e, carry):
        gout_ref[e] = mm(act_s[e], merged(every, 4 + e), TN).astype(BF)
        gin_ref[e] = mm(dhid_s[e], merged(every, e), TN).astype(BF)
        return carry

    lax.fori_loop(0, 4, forward, 0)
    scatter(
        outs, total, ring, z_out, z_in, ring_b, zb_in, z, y,
        (sz1, sz2), (sy1, sy2), (szb1, szb2), (syb1, syb2),
    )

    lane = lax.broadcasted_iota(jnp.int32, (8, EXTRA), 1)
    for a in range(8):
        val = total[a]
        if a < 4:
            extra = jnp.zeros((8, EXTRA), F32)
        else:
            mean = jnp.sum(blk[a - 4, :, :D] * val, 1, keepdims=True)
            extra = three(mean, lane, 0) + three(1.0 / blk[a - 4, :, D : D + 1], lane, 32)
        for j in range(IM):
            res[j, a : a + 1, :D] = val[j : j + 1]
            res[j, a : a + 1, D:] = extra[j : j + 1]
    for j in range(IM):
        resb[j] = res[j].astype(BF)
    give_back(resb, back, (bq1, bq2), (bj1, bj2))

    slots = back[...].astype(F32).reshape(cols, D + EXTRA).astype(BF)
    slot_rows, extra = slots[:, :D], slots[:, D:]
    which = lax.broadcasted_iota(jnp.int32, (8, EXTRA), 0)
    pick = (lax.broadcasted_iota(jnp.int32, (8, EXTRA), 1) >> 5) == which
    scalars = mm(jnp.where(pick, 1.0, 0.0).astype(BF), extra, NT)
    mean, den_inv = scalars[0:1], scalars[1:2]
    prods = mm(both_b, slot_rows, NT)
    dispatch = expo * den_inv
    taken = combine * prods[m:]
    dot = jnp.sum(jnp.where(first, taken, 0.0), 1, keepdims=True)
    dlog = jnp.where(first, taken - combine * dot, dispatch * (prods[:m] - mean))
    centre = jnp.sum(dlog * logits, 1, keepdims=True)
    pulled = (SCALE * dlog * col_inv).astype(BF)
    grad = mm(jnp.where(first, 0.0, dispatch).astype(BF), slot_rows)
    grad = grad + row_inv * (mm(pulled, params_b, NT) - x * (row_inv * centre))
    xs[...] = jnp.concatenate([grad, grad], 0).T
    low = lax.broadcasted_iota(jnp.int32, (1, 2 * m), 1) < m
    for e in range(NE):
        a, b, c = e * feats, e * feats + feats // 2, (e + 1) * feats
        chunk[e] = jnp.where(low, xs[a:b, :], xs[b:c, :]).astype(BF)
    finish = spread(chunk, y_in, (s2a, s2b))
    lax.fori_loop(0, 4, weight_grads, 0)
    finish()
    for j in range(IM):
        for h in (0, 1):
            a, b = y_in[4 * j + 2 * h].astype(F32), y_in[4 * j + 2 * h + 1].astype(F32)
            wide[h, pl.ds(j, feats // 2, IM), :] = jnp.where(left, a, pltpu.roll(b, 64, 1))
            wide[h, pl.ds(IM * (feats // 2) + j, feats // 2, IM), :] = jnp.where(
                left, pltpu.roll(a, 64, 1), b
            )
    for h in (0, 1):
        lanes = slice(128 * h, 128 * h + 128)
        y_ref[:, :, lanes] = wide[h].reshape(feats, IM, 128).astype(BF)


def whole(tgw, win, wout):
    feats, _, patches = tgw.shape
    lanes = patches // 2
    slots = 4 * NE
    cols = 2 * slots
    experts, f, d = win.shape
    dma = pltpu.SemaphoreType.DMA
    ring = dma((NZ, HALF + 1, 2))
    last = 8 - ZF

    def two(*shape):
        return [dma(shape), dma(shape)]

    block = (8, IM, d)
    vmem = pl.BlockSpec(memory_space=pltpu.VMEM)
    hbm = pl.BlockSpec(memory_space=pl.ANY)
    return pl.pallas_call(
        whole_kernel,
        out_shape=(
            jax.ShapeDtypeStruct((feats, IM, patches), BF),
            jax.ShapeDtypeStruct(win.shape, BF),
            jax.ShapeDtypeStruct(win.shape, BF),
        ),
        in_specs=[vmem, hbm, hbm],
        out_specs=(vmem,) * 3,
        scratch_shapes=[
            pltpu.VMEM((2, feats * IM, lanes), F32),
            pltpu.VMEM((2, feats * IM, lanes), F32),
            pltpu.VMEM((feats * IM, lanes), F32),
            pltpu.VMEM((NE, feats, lanes), BF),
            pltpu.VMEM((feats, cols), BF),
            pltpu.VMEM(win.shape, BF),
            pltpu.VMEM(win.shape, BF),
            pltpu.VMEM((NE, feats // 2, lanes), BF),
            pltpu.VMEM((NE, feats, lanes), BF),
            pltpu.VMEM((4, 8, feats, cols), BF),
            pltpu.VMEM((d, lanes), F32),
            pltpu.VMEM((d, cols), F32),
            pltpu.VMEM((4, IM, 8, d + EXTRA), BF),
            pltpu.VMEM((4, IM, 8, d + EXTRA), BF),
            pltpu.VMEM((IM, 8, d + EXTRA), BF),
            pltpu.VMEM((IM, 8, d + EXTRA), BF),
            pltpu.VMEM((8, IM, d + EXTRA), F32),
            pltpu.VMEM(block, BF),
            pltpu.VMEM((8, NZ * NY, IM, d), BF),
            pltpu.VMEM((8, NZ * NY, IM, d), BF),
            pltpu.VMEM((experts, NZ * NY * IM, f), BF),
            pltpu.VMEM((experts, NZ * NY * IM, f), BF),
            pltpu.VMEM((NZ, HALF, 2, ZF, IM, d), BF),
            pltpu.VMEM((NZ, ZF, IM, d), BF),
            pltpu.VMEM((NZ, ZF, IM, d), BF),
            pltpu.VMEM((HALF + 1, 2, last, IM, d), BF),
            pltpu.VMEM((NY, NZ, last, IM, d), BF),
            pltpu.VMEM(block, F32),
            pltpu.VMEM((IM, 8, d + EXTRA), F32),
            pltpu.VMEM((IM, 8, d + EXTRA), BF),
            pltpu.VMEM((4, IM, 8, d + EXTRA), BF),
            pltpu.VMEM((NE, feats // 2, lanes), BF),
            dma((2,)), *two(NE), *two(4), *two(8), *two(IM, 4), *two(IM),
            *two(NZ), ring, ring, *two(NY, NZ), *two(HALF + 1, 2),
            *two(NZ), ring, ring, *two(NY, NZ), *two(HALF + 1, 2),
            *two(IM, 4), *two(IM), *two(NE),
        ],
        compiler_params=pltpu.CompilerParams(
            collective_id=0, has_side_effects=True, vmem_limit_bytes=52 * 2**20
        ),
    )(tgw, win, wout)


def local(tokens, slot_params, w_in, w_out, out_grad):
    images, patches, feats = tokens.shape
    params = jnp.pad(slot_params, [(0, 0), (0, patches - slot_params.shape[1])])
    params = jnp.broadcast_to(params[:, None, :], (feats, images, patches))
    grad, grad_w_in, grad_w_out = whole(
        jnp.concatenate(
            [jnp.transpose(tokens, (2, 0, 1)), jnp.transpose(out_grad, (2, 0, 1)), params], 1
        ),
        jnp.swapaxes(w_in, 1, 2),
        w_out,
    )
    return (jnp.transpose(grad, (1, 2, 0)), jnp.swapaxes(grad_w_in, 1, 2), grad_w_out)


def solution(mesh):
    return jax.shard_map(
        local,
        mesh=mesh,
        in_specs=(
            P("dp", None, "expert"),
            P("expert", None),
            P("expert", None, "dp"),
            P("expert", "dp", None),
            P("dp", None, "expert"),
        ),
        out_specs=(P("dp", None, "expert"), P("expert", None, "dp"), P("expert", "dp", None)),
        check_vma=False,
    )
```
